512 devices in a mesh: ctx: 32 (over x, z), head: 16 (over y, core).
Axes of the slice: x: 4, y: 8, z: 8, core: 2. Of those that a mesh axis runs over, the one named last changes fastest.
Arguments:
- features: float32 [8192, 8192], P(('ctx', 'head')), may hold values from -6 to 6
- write_proj: float32 [8192, 512], P(('ctx', 'head')), may hold values from -2.5 to 2.5
- read_proj: float32 [8192, 512], P(('ctx', 'head')), may hold values from -2.5 to 2.5
- step_size: float32 [8192, 128], P(('ctx', 'head')), as said below
- decay_rate: float32 [128], P('head'), as said below
- skip_weight: float32 [128], P('head'), may hold values from 0.5 to 1.5
- upstream: float32 [8192, 8192], P(('ctx', 'head')), may hold values from -6 to 6
Outputs:
- features_grad: float32 [8192, 8192], P(('ctx', 'head'))
- write_grad: float32 [8192, 512], P(('ctx', 'head'))
- read_grad: float32 [8192, 512], P(('ctx', 'head'))
- step_grad: float32 [8192, 128], P(('ctx', 'head'))
The draws below stay inside these ranges and needn't reach their ends.
Inputs may be any that keep to these rules, and one draw needn't show every extreme that they name: `step_size`: every entry is positive. `decay_rate`: every entry is positive.
All inputs are finite; a program needn't handle non-finite values.
Results may differ from the reference program's by a relative error of at most 0.00018.
Values sent between devices are 32-bit elements; how exact they have to be, the bound alone decides.
A program may use at most 64 MiB of HBM per device.

```python
import math
import jax
import jax.numpy as jnp
from jax import lax

HEADS = 128
HEADDIM = 64
STATE = 128
GROUPS = 4
BLOCK = 128
SPAN_LENGTH = 8192


def head_rates(key, fast_share):
    key_base, key_pick, key_fast, key_slow = jax.random.split(key, 4)
    starting_amount = jnp.exp(jax.random.uniform(key_base, (HEADS,), jnp.float32, math.log(0.005), math.log(0.05)))
    pick = jax.random.uniform(key_pick, (HEADS,), jnp.float32)
    fast = jnp.exp(jax.random.uniform(key_fast, (HEADS,), jnp.float32, math.log(1.0 / 50.0), math.log(1.0 / 30.0)))
    slow = jnp.exp(jax.random.uniform(key_slow, (HEADS,), jnp.float32, math.log(0.1), math.log(0.5))) / SPAN_LENGTH
    rate = jnp.where(pick < fast_share, fast, slow)
    return (starting_amount, rate / starting_amount)


def draw_decay_rate(key, part):
    share = 0.5
    starting_amount, decay = head_rates(key, share)
    return decay


def draw_step_size(key, part):
    share = 0.5
    starting_amount, decay = head_rates(key, share)
    key = jax.random.fold_in(key, 3)
    key_rough, key_block, key_spot, key_loss = jax.random.split(key, 4)
    approximate_estimate = jax.random.uniform(key_rough, (SPAN_LENGTH, HEADS), jnp.float32, 0.5, 1.5)
    count = SPAN_LENGTH // BLOCK
    tier_sequence = jnp.exp(jax.random.uniform(key_block, (count, HEADS), jnp.float32, math.log(0.5), math.log(2.0)))
    tier_sequence = jnp.repeat(tier_sequence, BLOCK, axis=0)
    sample_offsets = jax.random.randint(key_spot, (3,), 0, SPAN_LENGTH)
    segment_sizes = jnp.any(jnp.arange(SPAN_LENGTH)[:, None] == sample_offsets[None, :], axis=1).astype(jnp.float32)
    losses = jax.random.uniform(key_loss, (HEADS,), jnp.float32, 0.22, 0.69)
    additional_summands = jnp.minimum(losses / decay, 1.0)
    return starting_amount[None, :] * approximate_estimate * tier_sequence + segment_sizes[:, None] * additional_summands[None, :]


def level_of(own_key, dims, cuts, low, top_value):
    factor_of = 1.0
    for axis_at, parts in cuts:
        draws = jax.random.uniform(jax.random.fold_in(jax.random.fold_in(own_key, 6), axis_at), (parts,), jnp.float32, low / len(cuts), top_value / len(cuts))
        factor_of = factor_of * jnp.repeat(jnp.exp(draws), dims[axis_at] // parts).reshape((-1,) + (1,) * (len(dims) - 1 - axis_at))
    return factor_of


def gaussian(own_key, shape, deviation, bound, cuts=(), kind=jnp.bfloat16):
    entries = deviation * jax.random.normal(own_key, shape, jnp.float32)
    if cuts:
        entries = entries * level_of(own_key, shape, cuts, -0.22, 0.18)
    return jnp.clip(entries, -bound, bound).astype(kind)


def setup_inputs(seed: int = 0) -> dict:
    streams_of = jax.random.split(jax.random.key(seed), 8)
    return {
        "features": gaussian(streams_of[0], (SPAN_LENGTH, HEADS * HEADDIM), 1.0, 6.0, ((0, 512),), jnp.float32),
        "write_proj": gaussian(streams_of[1], (SPAN_LENGTH, GROUPS * STATE), 0.3, 2.5, ((0, 512),), jnp.float32),
        "read_proj": gaussian(streams_of[2], (SPAN_LENGTH, GROUPS * STATE), 0.3, 2.5, ((0, 512),), jnp.float32),
        "step_size": draw_step_size(jax.random.fold_in(streams_of[7], 71), 0),
        "decay_rate": draw_decay_rate(jax.random.fold_in(streams_of[7], 71), 0),
        "skip_weight": jnp.clip(0.5 + 1.0 * jax.random.uniform(streams_of[5], (HEADS,), jnp.float32) ** level_of(streams_of[5], (HEADS,), ((0, 16),), -0.2, 0.2), 0.5, 1.5),
        "upstream": gaussian(streams_of[6], (SPAN_LENGTH, HEADS * HEADDIM), 1.0, 6.0, ((0, 512),), jnp.float32),
    }


def forward(features, write_proj, read_proj, step_size, decay_rate, skip_weight):
    high = lax.Precision.HIGHEST
    per_group = HEADS // GROUPS
    blocks = SPAN_LENGTH // BLOCK
    feats = features.reshape(blocks, BLOCK, HEADS, HEADDIM)
    writes = write_proj.reshape(blocks, BLOCK, GROUPS, STATE)
    reads = read_proj.reshape(blocks, BLOCK, GROUPS, STATE)
    steps = step_size.reshape(blocks, BLOCK, HEADS)
    positions = jnp.arange(BLOCK)
    lower = positions[:, None] >= positions[None, :]

    def block_step(carry, pieces):
        feat, write, read, step = pieces
        log_step = -step * decay_rate[None, :]
        cumul = jnp.cumsum(log_step, axis=0)
        scores = jnp.einsum('ign,jgn->gij', read, write, precision=high)
        scores = jnp.repeat(scores, per_group, axis=0)
        across = cumul.T
        gaps = across[:, :, None] - across[:, None, :]
        decays = jnp.where(lower[None], jnp.exp(jnp.where(lower[None], gaps, 0.0)), 0.0)
        mixing = scores * decays
        scaled = step[:, :, None] * feat
        inner = jnp.einsum('hij,jhp->ihp', mixing, scaled, precision=high)
        read_heads = jnp.repeat(read, per_group, axis=1)
        write_heads = jnp.repeat(write, per_group, axis=1)
        outer = jnp.exp(cumul)[:, :, None] * jnp.einsum('ihn,hnp->ihp', read_heads, carry, precision=high)
        result = inner + outer + skip_weight[None, :, None] * feat
        tail = jnp.exp(cumul[-1])
        weights = jnp.exp(cumul[-1][None, :] - cumul)
        written = jnp.einsum('jhn,jhp->hnp', write_heads * weights[:, :, None], scaled, precision=high)
        carry = tail[:, None, None] * carry + written
        return (carry, result)
    start = jnp.zeros((HEADS, STATE, HEADDIM), jnp.float32)
    final, outputs = lax.scan(jax.checkpoint(block_step), start, (feats, writes, reads, steps))
    return outputs.reshape(SPAN_LENGTH, HEADS * HEADDIM)

def reference(features, write_proj, read_proj, step_size, decay_rate, skip_weight, upstream):

    def mixer(feat_arg, write_arg, read_arg, step_arg):
        return forward(feat_arg, write_arg, read_arg, step_arg, decay_rate, skip_weight)
    primal, pullback = jax.vjp(mixer, features, write_proj, read_proj, step_size)
    grads = pullback(upstream)
    return (grads[0], grads[1], grads[2], grads[3])
```

```python
import functools

import jax
import jax.numpy as jnp
from jax import lax
from jax.experimental import pallas as pl
from jax.experimental.pallas import tpu as pltpu
from jax.sharding import PartitionSpec as P

STATE = 128
GROUPS = 4
WIDTH = 64
MESH = pl.DeviceIdType.MESH
F32 = jnp.float32
HIGH = lax.Precision.HIGH


def mm(a, b, dims, precision=HIGH):
    return lax.dot_general(
        a, b, (dims, ((), ())), precision=precision, preferred_element_type=F32
    )


def nn(a, b, precision=HIGH):
    return mm(a, b, ((1,), (0,)), precision)


def nt(a, b, precision=HIGH):
    return mm(a, b, ((1,), (1,)), precision)


def tn(a, b, precision=HIGH):
    return mm(a, b, ((0,), (0,)), precision)


def parts_of(a, count):
    out = []
    for _ in range(count):
        piece = a.astype(jnp.bfloat16)
        out.append(piece)
        a = a - piece.astype(F32)
    return out


def exact_nn(a, ones):
    n = a.shape[0]
    stacked = jnp.concatenate([p.astype(F32) for p in parts_of(a, 3)], axis=0)
    out = nn(stacked.astype(jnp.bfloat16), ones.astype(jnp.bfloat16), None)
    return (out[2 * n :] + out[n : 2 * n]) + out[:n]


def exact_tn(a, ones):
    stacked = jnp.concatenate([p.astype(F32) for p in parts_of(a, 3)][::-1], axis=0)
    tall = jnp.concatenate([ones] * 3, axis=0)
    return tn(stacked.astype(jnp.bfloat16), tall.astype(jnp.bfloat16), None)


def sum_nt(ones, b):
    ones = ones.astype(jnp.bfloat16)
    first, second = parts_of(b, 2)
    return nt(ones, second, None) + nt(ones, first, None)


class Unit:
    def __init__(self, index, scan, half, first, count, scanners):
        self.index, self.scan, self.half = index, scan, half
        self.first, self.count, self.share = first, count, count // scanners

    def cut(self):
        return slice(self.first, self.first + self.count)


class Exchange:
    def __init__(self, count, me, device, src, dst, sems, bulk):
        self.count, self.me, self.device = count, me, device
        self.src, self.dst, self.sems, self.bulk = src, dst, sems, bulk

    def start(self, to):
        pltpu.make_async_remote_copy(
            src_ref=self.src(to),
            dst_ref=self.dst(self.me),
            send_sem=self.sems.at[0],
            recv_sem=self.sems.at[1],
            device_id=self.device(to),
            device_id_type=MESH,
        ).start()

    def start_all(self):
        each(self.count, self.me, self.start)

    def whole(self, blocks):
        return pltpu.make_async_remote_copy(
            src_ref=self.bulk(blocks),
            dst_ref=self.bulk(blocks),
            send_sem=self.sems.at[0],
            recv_sem=self.sems.at[1],
            device_id=self.device(lax.rem(self.me + 1, self.count)),
            device_id_type=MESH,
        )

    def arrived(self, blocks=None):
        if self.count > 1:
            self.whole(blocks or self.count - 1).wait_recv()

    def sent(self, blocks=None):
        if self.count > 1:
            self.whole(blocks or self.count - 1).wait_send()


def each(count, me, act):
    if count % 2 == 0:
        act(lax.rem(me + count // 2, count))
    for j in range((count - 1) // 2, 0, -1):
        act(lax.rem(me + j, count))
        act(lax.rem(me + count - j, count))


def rows(index, size):
    return pl.ds(pl.multiple_of(index * size, size), size)


def kernel(
    nh, nx, nz, groups,
    rate_hbm, skip_hbm, x_hbm, dy_hbm, write_hbm, read_hbm, step_hbm,
    dx_ref, dwrite_ref, dread_ref, dstep_ref,
    rate_ref, skip_ref, write_ref, read_ref, step_ref,
    xg, dyg, bg, cg, pack_out, pack_in,
    cum_ref, wide_cum, grow, wide_step, wide_weight,
    decay_top, decay_low, score_top, score_low, grad_top, grad_low, row_sums,
    summed, dx_buf,
    locals_ref, scan_in, total_send, total_in, prefix, products, turned, ends,
    decay_out, decay_in, line_out, line_in,
    db_half, db_got, db_sum, db_in, dc_half, dc_got, dc_sum, dc_in,
    sems, pack_sems, own_sems,
):
    tok = step_ref.shape[0]
    heads = step_ref.shape[1]
    hl = heads // nh
    nc = nh // 2
    width = hl * WIDTH
    total = nh * tok
    low = total // 2
    pairs = hl // 2
    hh = hl // 2
    part = hh * WIDTH
    tail_rows = tok + hl
    me = lax.axis_index("head")
    at = lax.axis_index("ctx")
    my = me // 2
    core = lax.rem(me, 2)
    sibling = 1 - core
    mx = at // nz
    mz = lax.rem(at, nz)
    of_group = heads // groups

    def by_head(other):
        return {"head": other}

    def by_chip(other):
        return {"head": other * 2 + core}

    def by_core(other):
        return {"head": my * 2 + other}

    def by_z(other):
        return {"ctx": mx * nz + other}

    def by_x(other):
        return {"ctx": other * nz + mz}

    barrier = pltpu.get_barrier_semaphore()

    fetches = [
        pltpu.make_async_copy(src, dst, own_sems.at[3 + i])
        for i, (src, dst) in enumerate(
            (
                (step_hbm, step_ref),
                (write_hbm, write_ref),
                (read_hbm, read_ref),
                (rate_hbm, rate_ref),
                (skip_hbm, skip_ref),
            )
        )
    ]

    def greet(device):
        return lambda other: pl.semaphore_signal(
            barrier, inc=1, device_id=device(other), device_id_type=MESH
        )

    each(nh, me, greet(by_head))
    each(nz, mz, greet(by_z))
    if nx > 1:
        each(nx, mx, greet(by_x))
    for fetch in fetches:
        fetch.start()

    def columns(ref):
        return lambda other: ref.at[:, rows(other, width)]

    def some_columns(ref, first, size):
        return lambda other: ref.at[
            :, pl.ds(pl.multiple_of(other * width + first, size), size)
        ]

    def some_block(ref, first, size):
        return lambda other: ref.at[rows(other, tok), first : first + size]

    def block(ref, size):
        return lambda other: ref.at[rows(other, size), :]

    def along_head(src, dst, which, bulk):
        return Exchange(nh, me, by_head, src, dst, sems.at[which], bulk)

    def along_chip(src, dst, which, bulk):
        return Exchange(nc, my, by_chip, src, dst, sems.at[which], bulk)

    def across_core(src, dst, which, bulk):
        return Exchange(2, core, by_core, src, dst, sems.at[which], bulk)

    def first_rows(ref, size, cut=(0, None)):
        if cut[1] is None:
            return lambda n: ref.at[: n * size, :]
        return lambda n: ref.at[: n * size, cut[0] : cut[0] + cut[1]]

    halves = ((0, part), (part, part))
    ex_dy = [
        along_head(
            some_columns(dy_hbm, *cut), some_block(dyg, *cut), i, first_rows(dyg, tok, cut)
        )
        for i, cut in enumerate(halves)
    ]
    ex_dx = [
        along_head(
            some_block(dx_buf, *cut), some_columns(dx_ref, *cut), 2 + i,
            first_rows(dx_buf, tok, cut),
        )
        for i, cut in enumerate(halves)
    ]
    ex_x = [
        along_head(
            some_columns(x_hbm, *cut), some_block(xg, *cut), 4 + i, first_rows(xg, tok, cut)
        )
        for i, cut in enumerate(
            ((0, part), (part, part // 2), (part + part // 2, part // 2))
        )
    ]
    ex_db = along_chip(block(db_sum, tok), block(db_in, tok), 7, first_rows(db_in, tok))
    ex_dc = along_chip(
        block(dc_sum, tail_rows), block(dc_in, tail_rows), 8, first_rows(dc_in, tail_rows)
    )
    pair_pack = across_core(
        lambda t: pack_out.at[my], lambda s: pack_in.at[2 * my + s], 9, lambda n: pack_in.at[0]
    )
    pair_db = across_core(lambda t: db_half.at[t], lambda s: db_got, 10, lambda n: db_got)
    pair_dc = across_core(lambda t: dc_half.at[t], lambda s: dc_got, 11, lambda n: dc_got)
    relay = Exchange(
        nc, my, lambda t: by_core(sibling),
        lambda s: pack_in.at[2 * s + core], lambda s: None, sems.at[12],
        lambda n: pack_in.at[:n],
    )

    def pack_copy(to, slot):
        return pltpu.make_async_remote_copy(
            src_ref=pack_out.at[to],
            dst_ref=pack_in.at[2 * slot + core],
            send_sem=pack_sems.at[0],
            recv_sem=pack_sems.at[1 + slot],
            device_id=by_chip(to),
            device_id_type=MESH,
        )

    def packs_sent():
        if nc > 1:
            pltpu.make_async_remote_copy(
                src_ref=pack_out.at[: nc - 1],
                dst_ref=pack_out.at[: nc - 1],
                send_sem=pack_sems.at[0],
                recv_sem=pack_sems.at[1],
                device_id=by_chip(my),
                device_id_type=MESH,
            ).wait_send()

    grads_a = Unit(0, 1, 0, 0, part, hh)
    grads_b = Unit(1, 1, 1, part, part, hh)
    states_a = Unit(2, 0, 0, 0, part, hh)
    states_b = Unit(3, 0, 1, part, part // 2, hh)
    states_c = Unit(4, 0, 1, part + part // 2, part // 2, hh)
    my_half = lax.rem(mz, 2)

    def rows_of(u, i):
        return pl.ds(pl.multiple_of(u.first + i * u.share, u.share), u.share)

    def my_rows(u):
        return rows_of(u, mz // 2)

    def to_scanner(u):
        return Exchange(
            nz, mz, by_z,
            lambda t: locals_ref.at[u.scan, rows_of(u, t // 2), :],
            lambda s: scan_in.at[u.index, s, : u.share, :],
            sems.at[13 + u.index],
            lambda n: scan_in.at[u.index, :n, : u.share, :],
        )

    def from_scanner(u):
        return Exchange(
            nz, mz, by_z,
            lambda t: turned.at[u.index, t, : u.share, :],
            lambda s: ends.at[u.scan, my_rows(u), :],
            sems.at[18 + u.index],
            lambda n: turned.at[u.index, :n, : u.share, :],
        )

    def ex_total(u):
        return Exchange(
            nx, mx, by_x,
            lambda t: total_send.at[u.index, : u.share, :],
            lambda s: total_in.at[u.index, s, : u.share, :],
            sems.at[23 + u.index],
            lambda n: total_in.at[u.index, :n, : u.share, :],
        )

    ex_decay = Exchange(
        nz, mz, by_z, lambda t: decay_out, lambda s: decay_in.at[s], sems.at[28],
        lambda n: decay_in.at[:n],
    )
    ex_line_decay = Exchange(
        nx, mx, by_x, lambda t: line_out, lambda s: line_in.at[s], sems.at[29],
        lambda n: line_in.at[:n],
    )

    def by_half(half, act):
        @pl.when(my_half == half)
        def _():
            if hh > 1:
                act(hh - 1)

        @pl.when(my_half != half)
        def _():
            act(hh)

    def scanners(half, act):
        for j in range(hh):
            i = lax.rem(mz // 2 + hh // 2 + j, hh)

            @pl.when(2 * i + half != mz)
            def _(z=2 * i + half):
                act(z)

    own_dy = pltpu.make_async_copy(columns(dy_hbm)(me), block(dyg, tok)(me), own_sems.at[0])
    own_x = pltpu.make_async_copy(columns(x_hbm)(me), block(xg, tok)(me), own_sems.at[1])
    own_dy.start()
    own_x.start()
    for fetch in fetches:
        fetch.wait()
    padded = jnp.concatenate([step_ref[...], jnp.zeros((heads - tok, heads), F32)], axis=0)
    flipped = jnp.transpose(padded)
    for target in range(nc):
        g = target * 2 * hl // of_group
        pack_out[target, :tok, :] = write_ref[:, g * STATE : (g + 1) * STATE]
        pack_out[target, tok : 2 * tok, :] = read_ref[:, g * STATE : (g + 1) * STATE]
        first = target * 2 * hl
        pack_out[target, 2 * tok :, :heads] = flipped[first : first + hl, :] + pltpu.roll(
            flipped[first + hl : first + 2 * hl, :], tok, 1
        )
    pack_in[me] = pack_out[my]

    pl.semaphore_wait(barrier, (nh - 1) + (nz - 1) + (nx - 1))

    pair_pack.start(sibling)
    each(nc, my, lambda to: pack_copy(to, my).start())
    for exchange in ex_dy:
        exchange.start_all()

    def hand_on(chip):
        pack_copy(chip, chip).wait_recv()
        pltpu.make_async_remote_copy(
            src_ref=pack_in.at[2 * chip + core],
            dst_ref=pack_in.at[2 * chip + core],
            send_sem=sems.at[12, 0],
            recv_sem=sems.at[12, 1],
            device_id=by_core(sibling),
            device_id_type=MESH,
        ).start()

    each(nc, my, hand_on)
    for exchange in ex_x:
        exchange.start_all()
    pair_pack.arrived()
    relay.arrived()
    bg[...] = pack_in[:, :tok, :].reshape(total, STATE)
    cg[...] = pack_in[:, tok : 2 * tok, :].reshape(total, STATE)

    per_tile = heads // tok
    lane_h = lax.broadcasted_iota(jnp.int32, (hl, heads), 1) // tok
    tiles = []
    for first_source in range(0, nh, per_tile):
        tile = jnp.zeros((hl, heads), F32)
        for source in range(first_source, min(nh, first_source + per_tile)):
            spot = source - first_source
            piece = pack_in[source, 2 * tok :, :heads]
            both = []
            for c in range(2):
                shift = (heads + tok * (spot - c)) % heads
                both.append(pltpu.roll(piece, shift, 1) if shift else piece)
            tile = jnp.where(lane_h == spot, jnp.where(core == 0, both[0], both[1]), tile)
        tiles.append(tile)
    step = jnp.concatenate(tiles, axis=1)[:, :total]
    place = lax.broadcasted_iota(jnp.int32, (hl, 1), 0)
    rate = jnp.zeros((hl, 1), F32)
    for h in range(hl):
        rate = jnp.where(place == h, rate_ref[h], rate)
    lane = lax.broadcasted_iota(jnp.int32, (1, width), 1)
    skip = jnp.zeros((1, width), F32)
    for h in range(hl):
        skip = jnp.where(lane // WIDTH == h, skip_ref[h], skip)
    row_at = lax.broadcasted_iota(jnp.int32, (total, total), 0)
    col_at = lax.broadcasted_iota(jnp.int32, (total, total), 1)
    cumul = exact_nn(-step * rate, (col_at >= row_at).astype(F32))
    cum_ref[...] = cumul
    tail = jnp.exp(cumul[:, total - 1 : total])
    spread = (
        lax.broadcasted_iota(jnp.int32, (hl, width), 1) // WIDTH
        == lax.broadcasted_iota(jnp.int32, (hl, width), 0)
    ).astype(F32)
    wide = exact_tn(cumul, spread)
    wide_cum[...] = wide
    grow[...] = jnp.exp(wide)
    wide_weight[...] = jnp.exp(wide[total - 1 : total, :] - wide)
    wide_step[...] = exact_tn(step, spread)
    decay_out[...] = jnp.broadcast_to(tail, (hl, STATE))
    ex_decay.start_all()
    decay_in[mz] = decay_out[...]
    left_lanes = lax.broadcasted_iota(jnp.int32, (total, 2 * WIDTH), 1) < WIDTH
    later = lax.broadcasted_iota(jnp.int32, (low, low), 1) >= lax.broadcasted_iota(
        jnp.int32, (low, low), 0
    )

    def pair_cols(pair):
        return rows(pair, 2 * WIDTH)

    def masked(gap):
        return jnp.where(later, jnp.exp(jnp.where(later, gap, 0.0)), 0.0)

    def fill_decays(pair, carry):
        here = wide_cum[:, pair_cols(pair)]
        turned_round = pltpu.roll(here, WIDTH, 1)
        for side in range(2):
            h = 2 * pair + side
            col = jnp.where(left_lanes == (side == 0), here, turned_round)[:, :low]
            row = cum_ref[pl.ds(h, 1), :]
            decay_top[h, :, :low] = masked(row[:, :low] - col[:low, :])
            decay_top[h, :, low:] = jnp.exp(row[:, low:] - col[:low, :])
            decay_low[h] = masked(row[:, low:] - col[low:, :])
        return carry

    def send_local(u, local):
        locals_ref[u.scan, u.cut(), :] = local
        scanners(u.half, to_scanner(u).start)

        @pl.when(my_half == u.half)
        def _():
            scan_in[u.index, mz, : u.share, :] = locals_ref[u.scan, my_rows(u), :]

    def line_decays():
        ex_decay.arrived()
        product = decay_in[0]
        for z in range(1, nz):
            product = product * decay_in[z]
        line_out[...] = product
        line_in[mx] = product
        if nx > 1:
            ex_line_decay.start_all()
            ex_line_decay.arrived()

    def scan_line(u):
        @pl.when(my_half == u.half)
        def _():
            head = pl.ds((u.first + mz // 2 * u.share) // WIDTH, 1)
            to_scanner(u).arrived()
            state = jnp.zeros((u.share, STATE), F32)
            product = jnp.ones((1, STATE), F32)
            for lap in range(nz):
                z = nz - 1 - lap if u.scan else lap
                prefix[u.index, z, : u.share, :] = state
                products[u.index, z] = jnp.broadcast_to(product, (8, STATE))
                factor = decay_in[z, head, :]
                state = factor * state + scan_in[u.index, z, : u.share, :]
                product = product * factor
            total_send[u.index, : u.share, :] = state
            if nx > 1:
                ex_total(u).start_all()

    def scan_turn(u):
        @pl.when(my_half == u.half)
        def _():
            head = pl.ds((u.first + mz // 2 * u.share) // WIDTH, 1)
            state = jnp.zeros((u.share, STATE), F32)
            if nx > 1:
                total_in[u.index, mx, : u.share, :] = total_send[u.index, : u.share, :]
                ex_total(u).arrived()
                for lap in range(nx):
                    x = nx - 1 - lap if u.scan else lap
                    before = x > mx if u.scan else x < mx
                    moved = line_in[x, head, :] * state + total_in[u.index, x, : u.share, :]
                    state = jnp.where(before, moved, state)

            def turn(z):
                turned[u.index, z, : u.share, :] = (
                    prefix[u.index, z, : u.share, :] + products[u.index, z, :1, :] * state
                )

            def turn_to(z):
                turn(z)
                from_scanner(u).start(z)

            each(nz, mz, turn_to)
            turn(mz)
            ends[u.scan, my_rows(u), :] = turned[u.index, mz, : u.share, :]

    def scan_arrived(u):
        by_half(u.half, from_scanner(u).arrived)

    def scan_sent(u):
        by_half(u.half, to_scanner(u).sent)

        @pl.when(my_half == u.half)
        def _():
            ex_total(u).sent()
            from_scanner(u).sent()

    def send_grad(u):
        cols = u.cut()
        ex_dy[u.half].arrived()
        send_local(u, tn(grow[:, cols] * dyg[:, cols], cg[...]))

    def send_state(u):
        cols = u.cut()
        ex_x[u.index - 2].arrived()
        send_local(u, tn(wide_weight[:, cols] * wide_step[:, cols] * xg[:, cols], bg[...]))

    def send_dx(u):
        scan_arrived(u)
        cols = u.cut()
        whole = summed[:, cols] + wide_weight[:, cols] * nt(bg[...], ends[1, cols, :])
        summed[:, cols] = whole
        dx_buf[:, cols] = wide_step[:, cols] * whole + skip[:, cols] * dyg[:, cols]
        ex_dx[u.half].start_all()

    own_dy.wait()
    send_grad(grads_a)
    score_top[...] = nt(bg[:low, :], cg[...])
    score_low[...] = nt(bg[low:, :], cg[low:, :])
    lax.fori_loop(0, pairs, fill_decays, 0)

    def fill_summed(pair, carry):
        cols = pair_cols(pair)
        grads = dyg[:, cols]
        above, below = [], []
        for side in range(2):
            h = 2 * pair + side
            above.append(nn(score_top[...] * decay_top[h], grads))
            below.append(nn(score_low[...] * decay_low[h], grads[low:, :]))
        summed[:low, cols] = jnp.where(left_lanes[:low, :], above[0], above[1])
        summed[low:, cols] = jnp.where(left_lanes[:low, :], below[0], below[1])
        return carry

    def fill_grad_score(pair, carry):
        cols = pair_cols(pair)
        grads = dyg[:, cols]
        scaled = wide_step[:, cols] * xg[:, cols]
        for side in range(2):
            h = 2 * pair + side
            one = jnp.where(left_lanes == (side == 0), scaled, 0.0)
            above = nt(one[:low, :], grads) * decay_top[h]
            below = nt(one[low:, :], grads[low:, :]) * decay_low[h]
            grad_top[...] += above
            grad_low[...] += below
            sums = jnp.sum(above * score_top[...], axis=0, keepdims=True)
            more = jnp.sum(below * score_low[...], axis=0, keepdims=True)
            mine = lax.broadcasted_iota(jnp.int32, (hl, low), 0) == h
            row_sums[:, :low] += jnp.where(mine, sums[:, :low], 0.0)
            row_sums[:, low:] += jnp.where(mine, sums[:, low:] + more, 0.0)
        return carry

    grad_top[...] = jnp.zeros_like(grad_top)
    grad_low[...] = jnp.zeros_like(grad_low)
    row_sums[...] = jnp.zeros_like(row_sums)
    line_decays()
    send_grad(grads_b)
    lax.fori_loop(0, pairs // 2, fill_summed, 0)
    scan_line(grads_a)
    own_x.wait()
    send_state(states_a)
    scan_turn(grads_a)
    scan_line(grads_b)
    send_state(states_b)
    send_state(states_c)
    lax.fori_loop(pairs // 2, pairs, fill_summed, 0)
    scan_turn(grads_b)
    scan_line(states_a)
    send_dx(grads_a)
    scan_turn(states_a)
    scan_line(states_b)
    scan_line(states_c)
    lax.fori_loop(0, pairs // 2, fill_grad_score, 0)
    scan_turn(states_b)
    scan_turn(states_c)
    send_dx(grads_b)
    lax.fori_loop(pairs // 2, pairs, fill_grad_score, 0)
    end = ends[1]
    along = sum_nt(spread, xg[...] * summed[...])

    def by_target_core(half, stride, first, value):
        size = value.shape[0] // nh
        for target in range(nh):
            base = (target // 2) * stride + first
            half[target % 2, base : base + size, :] = value[target * size : (target + 1) * size, :]

    from_states = nn(wide_weight[...] * wide_step[...] * xg[...], end)
    by_target_core(db_half, tok, 0, from_states + jnp.concatenate(
        [nn(grad_top[...], cg[...]), nn(grad_low[...], cg[low:, :])], axis=0
    ))
    pair_db.start(sibling)
    from_score = jnp.concatenate(
        [
            tn(grad_top[:, :low], bg[:low, :]),
            tn(grad_top[:, low:], bg[:low, :]) + tn(grad_low[...], bg[low:, :]),
        ],
        axis=0,
    )
    outer = grow[...] * dyg[...]
    made = jnp.sum((end * locals_ref[0]).reshape(hl, WIDTH, STATE), axis=1)
    read_part = from_score
    along_read = row_sums[...] - step * along
    for u in (states_a, states_b, states_c):
        scan_arrived(u)
        start = ends[0, u.cut(), :]
        read_part = read_part + nn(outer[:, u.cut()], start)
        along_read = along_read + sum_nt(
            spread[:, u.cut()], outer[:, u.cut()] * nt(cg[...], start)
        )
    by_target_core(dc_half, tail_rows, 0, read_part)
    kept = jnp.sum((end * ends[0]).reshape(hl, WIDTH, STATE), axis=1)
    last = jnp.sum(tail * kept + made, axis=1, keepdims=True)
    lane_t = lax.broadcasted_iota(jnp.int32, (hl, total), 1)
    grad_cum = along_read + jnp.where(lane_t == total - 1, last, 0.0)
    grad_log = exact_nn(grad_cum, (row_at >= col_at).astype(F32))
    grad_step = along - rate * grad_log
    for target in range(nh):
        tile = target // per_tile
        begin = tile * heads
        piece = grad_step[:, begin : min(total, begin + heads)]
        if piece.shape[1] < heads:
            piece = jnp.concatenate(
                [piece, jnp.zeros((hl, heads - piece.shape[1]), F32)], axis=1
            )
        placed = []
        for c in range(2):
            shift = (heads + tok * c - tok * (target - tile * per_tile)) % heads
            placed.append(pltpu.roll(piece, shift, 1) if shift else piece)
        base = (target // 2) * tail_rows + tok
        dc_half[target % 2, base : base + hl, :heads] = jnp.where(
            lane_h == core, jnp.where(core == 0, placed[0], placed[1]), 0.0
        )
    pair_dc.start(sibling)
    pair_db.arrived()
    db_sum[...] = db_half[core] + db_got[...]
    ex_db.start_all()
    db_in[rows(my, tok), :] = db_sum[rows(my, tok), :]
    pair_dc.arrived()
    dc_sum[...] = dc_half[core] + dc_got[...]
    ex_dc.start_all()
    dc_in[rows(my, tail_rows), :] = dc_sum[rows(my, tail_rows), :]

    share = nc // groups

    def fold(received, stride, out):
        for g in range(groups):
            part = received[g * share * stride : g * share * stride + tok, :]
            for s in range(g * share + 1, (g + 1) * share):
                part = part + received[s * stride : s * stride + tok, :]
            out[:, g * STATE : (g + 1) * STATE] = part

    dx_ref[:, rows(me, width)] = dx_buf[rows(me, tok), :]
    for exchange in (*ex_dy, *ex_x, *ex_dx, relay, ex_decay, ex_line_decay):
        exchange.sent()
    packs_sent()
    for u in (grads_a, grads_b, states_a, states_b, states_c):
        scan_sent(u)
    for exchange in (pair_pack, pair_db, pair_dc):
        exchange.sent()
    for exchange in ex_dx:
        exchange.arrived()
    ex_db.arrived()
    fold(db_in, tok, dwrite_ref)
    ex_db.sent()
    ex_dc.arrived()
    fold(dc_in, tail_rows, dread_ref)
    by_heads = []
    for chip in range(nc):
        piece = dc_in[chip * tail_rows + tok : (chip + 1) * tail_rows, :heads]
        by_heads += [piece, pltpu.roll(piece, heads - tok, 1)]
    dstep_ref[...] = jnp.transpose(jnp.concatenate(by_heads, axis=0))[:tok, :]
    ex_dc.sent()


def hand_out(count, *refs):
    for i in range(count):
        refs[count + i][...] = refs[i][...]


def on_device(groups, features, write_proj, read_proj, step_size, decay_rate, skip_weight, upstream):
    nh = lax.axis_size("head")
    tok, heads = step_size.shape
    hl = heads // nh
    nz = hl
    nx = lax.axis_size("ctx") // nz
    width = hl * WIDTH
    nc = nh // 2
    total = nh * tok
    low = total // 2
    vmem = pl.BlockSpec(memory_space=pltpu.VMEM)
    hbm = pl.BlockSpec(memory_space=pltpu.HBM)

    def buf(*shape):
        return pltpu.VMEM(shape, F32)

    results = pl.pallas_call(
        functools.partial(kernel, nh, nx, nz, groups),
        out_shape=(
            jax.ShapeDtypeStruct(features.shape, F32),
            jax.ShapeDtypeStruct(write_proj.shape, F32),
            jax.ShapeDtypeStruct(read_proj.shape, F32),
            jax.ShapeDtypeStruct(step_size.shape, F32),
        ),
        in_specs=[hbm] * 7,
        out_specs=(vmem, vmem, vmem, vmem),
        scratch_shapes=[
            pltpu.SMEM(decay_rate.shape, F32),
            pltpu.SMEM(skip_weight.shape, F32),
            buf(*write_proj.shape),
            buf(*read_proj.shape),
            buf(*step_size.shape),
            buf(total, width),
            buf(total, width),
            buf(total, STATE),
            buf(total, STATE),
            buf(nc, 2 * tok + hl, STATE),
            buf(nh, 2 * tok + hl, STATE),
            buf(hl, total),
            buf(total, width),
            buf(total, width),
            buf(total, width),
            buf(total, width),
            buf(hl, low, total),
            buf(hl, low, low),
            buf(low, total),
            buf(low, low),
            buf(low, total),
            buf(low, low),
            buf(hl, total),
            buf(total, width),
            buf(total, width),
            buf(2, hl * WIDTH, STATE),
            buf(5, nz, WIDTH, STATE),
            buf(5, WIDTH, STATE),
            buf(5, nx, WIDTH, STATE),
            buf(5, nz, WIDTH, STATE),
            buf(5, nz, 8, STATE),
            buf(5, nz, WIDTH, STATE),
            buf(2, hl * WIDTH, STATE),
            buf(hl, STATE),
            buf(nz, hl, STATE),
            buf(hl, STATE),
            buf(nx, hl, STATE),
            buf(2, nc * tok, STATE),
            buf(nc * tok, STATE),
            buf(nc * tok, STATE),
            buf(nc * tok, STATE),
            buf(2, nc * (tok + hl), STATE),
            buf(nc * (tok + hl), STATE),
            buf(nc * (tok + hl), STATE),
            buf(nc * (tok + hl), STATE),
            pltpu.SemaphoreType.DMA((30, 2)),
            pltpu.SemaphoreType.DMA((1 + nc,)),
            pltpu.SemaphoreType.DMA((8,)),
        ],
        compiler_params=pltpu.CompilerParams(
            collective_id=0, has_side_effects=True, vmem_limit_bytes=64 * 1024 * 1024
        ),
        cost_estimate=pl.CostEstimate(
            flops=1_200_000_000, bytes_accessed=8_000_000, transcendentals=600_000
        ),
    )(decay_rate, skip_weight, features, upstream, write_proj, read_proj, step_size)
    return pl.pallas_call(
        functools.partial(hand_out, len(results)),
        out_shape=tuple(jax.ShapeDtypeStruct(r.shape, F32) for r in results),
        in_specs=[vmem] * len(results),
        out_specs=(vmem,) * len(results),
        compiler_params=pltpu.CompilerParams(vmem_limit_bytes=64 * 1024 * 1024),
        cost_estimate=pl.CostEstimate(flops=0, bytes_accessed=1_200_000, transcendentals=0),
    )(*results)


def solution(mesh):
    tokens = P(("ctx", "head"), None)
    return jax.shard_map(
        functools.partial(on_device, GROUPS),
        mesh=mesh,
        in_specs=(tokens, tokens, tokens, tokens, P("head"), P("head"), tokens),
        out_specs=(tokens, tokens, tokens, tokens),
        check_vma=False,
    )
```

```python
import functools

import jax
import jax.numpy as jnp
from jax import lax
from jax.experimental import pallas as pl
from jax.experimental.pallas import tpu as pltpu
from jax.sharding import PartitionSpec as P

STATE = 128
GROUPS = 4
WIDTH = 64
MESH = pl.DeviceIdType.MESH
F32 = jnp.float32
HIGH = lax.Precision.HIGH


def mm(a, b, dims, precision=HIGH):
    return lax.dot_general(
        a, b, (dims, ((), ())), precision=precision, preferred_element_type=F32
    )


def nn(a, b, precision=HIGH):
    return mm(a, b, ((1,), (0,)), precision)


def nt(a, b, precision=HIGH):
    return mm(a, b, ((1,), (1,)), precision)


def tn(a, b, precision=HIGH):
    return mm(a, b, ((0,), (0,)), precision)


def parts_of(a, count):
    out = []
    for _ in range(count):
        piece = a.astype(jnp.bfloat16)
        out.append(piece)
        a = a - piece.astype(F32)
    return out


def exact_nn(a, ones):
    n = a.shape[0]
    stacked = jnp.concatenate([p.astype(F32) for p in parts_of(a, 3)], axis=0)
    out = nn(stacked.astype(jnp.bfloat16), ones.astype(jnp.bfloat16), None)
    return (out[2 * n :] + out[n : 2 * n]) + out[:n]


def exact_tn(a, ones):
    stacked = jnp.concatenate([p.astype(F32) for p in parts_of(a, 3)][::-1], axis=0)
    tall = jnp.concatenate([ones] * 3, axis=0)
    return tn(stacked.astype(jnp.bfloat16), tall.astype(jnp.bfloat16), None)


def sum_nt(ones, b):
    ones = ones.astype(jnp.bfloat16)
    first, second = parts_of(b, 2)
    return nt(ones, second, None) + nt(ones, first, None)


class Unit:
    def __init__(self, index, scan, half, first, count, scanners):
        self.index, self.scan, self.half = index, scan, half
        self.first, self.count, self.share = first, count, count // scanners

    def cut(self):
        return slice(self.first, self.first + self.count)


class Exchange:
    def __init__(self, count, me, device, src, dst, sems, bulk):
        self.count, self.me, self.device = count, me, device
        self.src, self.dst, self.sems, self.bulk = src, dst, sems, bulk

    def start(self, to):
        pltpu.make_async_remote_copy(
            src_ref=self.src(to),
            dst_ref=self.dst(self.me),
            send_sem=self.sems.at[0],
            recv_sem=self.sems.at[1],
            device_id=self.device(to),
            device_id_type=MESH,
        ).start()

    def start_all(self):
        each(self.count, self.me, self.start)

    def whole(self, blocks):
        return pltpu.make_async_remote_copy(
            src_ref=self.bulk(blocks),
            dst_ref=self.bulk(blocks),
            send_sem=self.sems.at[0],
            recv_sem=self.sems.at[1],
            device_id=self.device(lax.rem(self.me + 1, self.count)),
            device_id_type=MESH,
        )

    def arrived(self, blocks=None):
        if self.count > 1:
            self.whole(blocks or self.count - 1).wait_recv()

    def sent(self, blocks=None):
        if self.count > 1:
            self.whole(blocks or self.count - 1).wait_send()


def each(count, me, act):
    if count % 2 == 0:
        act(lax.rem(me + count // 2, count))
    for j in range((count - 1) // 2, 0, -1):
        act(lax.rem(me + j, count))
        act(lax.rem(me + count - j, count))


def rows(index, size):
    return pl.ds(pl.multiple_of(index * size, size), size)


def kernel(
    nh, nx, nz, groups,
    rate_hbm, skip_hbm, x_hbm, dy_hbm, write_hbm, read_hbm, step_hbm,
    dx_hbm, dwrite_ref, dread_ref, dstep_ref,
    rate_ref, skip_ref, write_ref, read_ref, step_ref,
    xg, dyg, bg, cg, pack_out, pack_in,
    cum_ref, wide_cum, grow, wide_step, wide_weight,
    decay_top, decay_low, score_top, score_low, grad_top, grad_low, row_sums,
    summed, dx_buf, dx_ref,
    locals_ref, scan_in, total_send, total_in, prefix, products, turned, ends,
    decay_out, decay_in, line_out, line_in,
    db_half, db_got, db_sum, db_in, dc_half, dc_got, dc_sum, dc_in,
    sems, pack_sems, own_sems,
):
    tok = step_ref.shape[0]
    heads = step_ref.shape[1]
    hl = heads // nh
    nc = nh // 2
    width = hl * WIDTH
    total = nh * tok
    low = total // 2
    pairs = hl // 2
    hh = hl // 2
    part = hh * WIDTH
    tail_rows = tok + hl
    me = lax.axis_index("head")
    at = lax.axis_index("ctx")
    my = me // 2
    core = lax.rem(me, 2)
    sibling = 1 - core
    mx = at // nz
    mz = lax.rem(at, nz)
    of_group = heads // groups

    def by_head(other):
        return {"head": other}

    def by_chip(other):
        return {"head": other * 2 + core}

    def by_core(other):
        return {"head": my * 2 + other}

    def by_z(other):
        return {"ctx": mx * nz + other}

    def by_x(other):
        return {"ctx": other * nz + mz}

    barrier = pltpu.get_barrier_semaphore()

    fetches = [
        pltpu.make_async_copy(src, dst, own_sems.at[3 + i])
        for i, (src, dst) in enumerate(
            (
                (step_hbm, step_ref),
                (write_hbm, write_ref),
                (read_hbm, read_ref),
                (rate_hbm, rate_ref),
                (skip_hbm, skip_ref),
            )
        )
    ]

    def greet(device):
        return lambda other: pl.semaphore_signal(
            barrier, inc=1, device_id=device(other), device_id_type=MESH
        )

    each(nh, me, greet(by_head))
    each(nz, mz, greet(by_z))
    if nx > 1:
        each(nx, mx, greet(by_x))
    for fetch in fetches:
        fetch.start()

    def columns(ref):
        return lambda other: ref.at[:, rows(other, width)]

    def some_columns(ref, first, size):
        return lambda other: ref.at[
            :, pl.ds(pl.multiple_of(other * width + first, size), size)
        ]

    def some_block(ref, first, size):
        return lambda other: ref.at[rows(other, tok), first : first + size]

    def block(ref, size):
        return lambda other: ref.at[rows(other, size), :]

    def along_head(src, dst, which, bulk):
        return Exchange(nh, me, by_head, src, dst, sems.at[which], bulk)

    def along_chip(src, dst, which, bulk):
        return Exchange(nc, my, by_chip, src, dst, sems.at[which], bulk)

    def across_core(src, dst, which, bulk):
        return Exchange(2, core, by_core, src, dst, sems.at[which], bulk)

    def first_rows(ref, size, cut=(0, None)):
        if cut[1] is None:
            return lambda n: ref.at[: n * size, :]
        return lambda n: ref.at[: n * size, cut[0] : cut[0] + cut[1]]

    halves = ((0, part), (part, part))
    ex_dy = [
        along_head(
            some_columns(dy_hbm, *cut), some_block(dyg, *cut), i, first_rows(dyg, tok, cut)
        )
        for i, cut in enumerate(halves)
    ]
    ex_dx = [
        along_head(
            some_block(dx_buf, *cut), some_columns(dx_ref, *cut), 2 + i,
            first_rows(dx_buf, tok, cut),
        )
        for i, cut in enumerate(halves)
    ]
    ex_x = [
        along_head(
            some_columns(x_hbm, *cut), some_block(xg, *cut), 4 + i, first_rows(xg, tok, cut)
        )
        for i, cut in enumerate(
            ((0, part), (part, part // 2), (part + part // 2, part // 2))
        )
    ]
    ex_db = along_chip(block(db_sum, tok), block(db_in, tok), 7, first_rows(db_in, tok))
    ex_dc = along_chip(
        block(dc_sum, tail_rows), block(dc_in, tail_rows), 8, first_rows(dc_in, tail_rows)
    )
    pair_pack = across_core(
        lambda t: pack_out.at[my], lambda s: pack_in.at[2 * my + s], 9, lambda n: pack_in.at[0]
    )
    pair_db = across_core(lambda t: db_half.at[t], lambda s: db_got, 10, lambda n: db_got)
    pair_dc = across_core(lambda t: dc_half.at[t], lambda s: dc_got, 11, lambda n: dc_got)
    relay = Exchange(
        nc, my, lambda t: by_core(sibling),
        lambda s: pack_in.at[2 * s + core], lambda s: None, sems.at[12],
        lambda n: pack_in.at[:n],
    )

    def pack_copy(to, slot):
        return pltpu.make_async_remote_copy(
            src_ref=pack_out.at[to],
            dst_ref=pack_in.at[2 * slot + core],
            send_sem=pack_sems.at[0],
            recv_sem=pack_sems.at[1 + slot],
            device_id=by_chip(to),
            device_id_type=MESH,
        )

    def packs_sent():
        if nc > 1:
            pltpu.make_async_remote_copy(
                src_ref=pack_out.at[: nc - 1],
                dst_ref=pack_out.at[: nc - 1],
                send_sem=pack_sems.at[0],
                recv_sem=pack_sems.at[1],
                device_id=by_chip(my),
                device_id_type=MESH,
            ).wait_send()

    grads_a = Unit(0, 1, 0, 0, part, hh)
    grads_b = Unit(1, 1, 1, part, part, hh)
    states_a = Unit(2, 0, 0, 0, part, hh)
    states_b = Unit(3, 0, 1, part, part // 2, hh)
    states_c = Unit(4, 0, 1, part + part // 2, part // 2, hh)
    my_half = lax.rem(mz, 2)

    def rows_of(u, i):
        return pl.ds(pl.multiple_of(u.first + i * u.share, u.share), u.share)

    def my_rows(u):
        return rows_of(u, mz // 2)

    def to_scanner(u):
        return Exchange(
            nz, mz, by_z,
            lambda t: locals_ref.at[u.scan, rows_of(u, t // 2), :],
            lambda s: scan_in.at[u.index, s, : u.share, :],
            sems.at[13 + u.index],
            lambda n: scan_in.at[u.index, :n, : u.share, :],
        )

    def from_scanner(u):
        return Exchange(
            nz, mz, by_z,
            lambda t: turned.at[u.index, t, : u.share, :],
            lambda s: ends.at[u.scan, my_rows(u), :],
            sems.at[18 + u.index],
            lambda n: turned.at[u.index, :n, : u.share, :],
        )

    def ex_total(u):
        return Exchange(
            nx, mx, by_x,
            lambda t: total_send.at[u.index, : u.share, :],
            lambda s: total_in.at[u.index, s, : u.share, :],
            sems.at[23 + u.index],
            lambda n: total_in.at[u.index, :n, : u.share, :],
        )

    ex_decay = Exchange(
        nz, mz, by_z, lambda t: decay_out, lambda s: decay_in.at[s], sems.at[28],
        lambda n: decay_in.at[:n],
    )
    ex_line_decay = Exchange(
        nx, mx, by_x, lambda t: line_out, lambda s: line_in.at[s], sems.at[29],
        lambda n: line_in.at[:n],
    )

    def by_half(half, act):
        @pl.when(my_half == half)
        def _():
            if hh > 1:
                act(hh - 1)

        @pl.when(my_half != half)
        def _():
            act(hh)

    def scanners(half, act):
        for j in range(hh):
            i = lax.rem(mz // 2 + hh // 2 + j, hh)

            @pl.when(2 * i + half != mz)
            def _(z=2 * i + half):
                act(z)

    own_dy = pltpu.make_async_copy(columns(dy_hbm)(me), block(dyg, tok)(me), own_sems.at[0])
    own_x = pltpu.make_async_copy(columns(x_hbm)(me), block(xg, tok)(me), own_sems.at[1])
    own_dy.start()
    own_x.start()
    for fetch in fetches:
        fetch.wait()
    padded = jnp.concatenate([step_ref[...], jnp.zeros((heads - tok, heads), F32)], axis=0)
    flipped = jnp.transpose(padded)
    for target in range(nc):
        g = target * 2 * hl // of_group
        pack_out[target, :tok, :] = write_ref[:, g * STATE : (g + 1) * STATE]
        pack_out[target, tok : 2 * tok, :] = read_ref[:, g * STATE : (g + 1) * STATE]
        first = target * 2 * hl
        pack_out[target, 2 * tok :, :heads] = flipped[first : first + hl, :] + pltpu.roll(
            flipped[first + hl : first + 2 * hl, :], tok, 1
        )
    pack_in[me] = pack_out[my]

    pl.semaphore_wait(barrier, (nh - 1) + (nz - 1) + (nx - 1))

    pair_pack.start(sibling)
    each(nc, my, lambda to: pack_copy(to, my).start())
    for exchange in ex_dy:
        exchange.start_all()

    def hand_on(chip):
        pack_copy(chip, chip).wait_recv()
        pltpu.make_async_remote_copy(
            src_ref=pack_in.at[2 * chip + core],
            dst_ref=pack_in.at[2 * chip + core],
            send_sem=sems.at[12, 0],
            recv_sem=sems.at[12, 1],
            device_id=by_core(sibling),
            device_id_type=MESH,
        ).start()

    each(nc, my, hand_on)
    for exchange in ex_x:
        exchange.start_all()
    pair_pack.arrived()
    relay.arrived()
    bg[...] = pack_in[:, :tok, :].reshape(total, STATE)
    cg[...] = pack_in[:, tok : 2 * tok, :].reshape(total, STATE)

    per_tile = heads // tok
    lane_h = lax.broadcasted_iota(jnp.int32, (hl, heads), 1) // tok
    tiles = []
    for first_source in range(0, nh, per_tile):
        tile = jnp.zeros((hl, heads), F32)
        for source in range(first_source, min(nh, first_source + per_tile)):
            spot = source - first_source
            piece = pack_in[source, 2 * tok :, :heads]
            both = []
            for c in range(2):
                shift = (heads + tok * (spot - c)) % heads
                both.append(pltpu.roll(piece, shift, 1) if shift else piece)
            tile = jnp.where(lane_h == spot, jnp.where(core == 0, both[0], both[1]), tile)
        tiles.append(tile)
    step = jnp.concatenate(tiles, axis=1)[:, :total]
    place = lax.broadcasted_iota(jnp.int32, (hl, 1), 0)
    rate = jnp.zeros((hl, 1), F32)
    for h in range(hl):
        rate = jnp.where(place == h, rate_ref[h], rate)
    lane = lax.broadcasted_iota(jnp.int32, (1, width), 1)
    skip = jnp.zeros((1, width), F32)
    for h in range(hl):
        skip = jnp.where(lane // WIDTH == h, skip_ref[h], skip)
    row_at = lax.broadcasted_iota(jnp.int32, (total, total), 0)
    col_at = lax.broadcasted_iota(jnp.int32, (total, total), 1)
    cumul = exact_nn(-step * rate, (col_at >= row_at).astype(F32))
    cum_ref[...] = cumul
    tail = jnp.exp(cumul[:, total - 1 : total])
    spread = (
        lax.broadcasted_iota(jnp.int32, (hl, width), 1) // WIDTH
        == lax.broadcasted_iota(jnp.int32, (hl, width), 0)
    ).astype(F32)
    wide = exact_tn(cumul, spread)
    wide_cum[...] = wide
    grow[...] = jnp.exp(wide)
    wide_weight[...] = jnp.exp(wide[total - 1 : total, :] - wide)
    wide_step[...] = exact_tn(step, spread)
    decay_out[...] = jnp.broadcast_to(tail, (hl, STATE))
    ex_decay.start_all()
    decay_in[mz] = decay_out[...]
    left_lanes = lax.broadcasted_iota(jnp.int32, (total, 2 * WIDTH), 1) < WIDTH
    later = lax.broadcasted_iota(jnp.int32, (low, low), 1) >= lax.broadcasted_iota(
        jnp.int32, (low, low), 0
    )

    def pair_cols(pair):
        return rows(pair, 2 * WIDTH)

    def masked(gap):
        return jnp.where(later, jnp.exp(jnp.where(later, gap, 0.0)), 0.0)

    def fill_decays(pair, carry):
        here = wide_cum[:, pair_cols(pair)]
        turned_round = pltpu.roll(here, WIDTH, 1)
        for side in range(2):
            h = 2 * pair + side
            col = jnp.where(left_lanes == (side == 0), here, turned_round)[:, :low]
            row = cum_ref[pl.ds(h, 1), :]
            decay_top[h, :, :low] = masked(row[:, :low] - col[:low, :])
            decay_top[h, :, low:] = jnp.exp(row[:, low:] - col[:low, :])
            decay_low[h] = masked(row[:, low:] - col[low:, :])
        return carry

    def send_local(u, local):
        locals_ref[u.scan, u.cut(), :] = local
        scanners(u.half, to_scanner(u).start)

        @pl.when(my_half == u.half)
        def _():
            scan_in[u.index, mz, : u.share, :] = locals_ref[u.scan, my_rows(u), :]

    def line_decays():
        ex_decay.arrived()
        product = decay_in[0]
        for z in range(1, nz):
            product = product * decay_in[z]
        line_out[...] = product
        line_in[mx] = product
        if nx > 1:
            ex_line_decay.start_all()
            ex_line_decay.arrived()

    def scan_line(u):
        @pl.when(my_half == u.half)
        def _():
            head = pl.ds((u.first + mz // 2 * u.share) // WIDTH, 1)
            to_scanner(u).arrived()
            state = jnp.zeros((u.share, STATE), F32)
            product = jnp.ones((1, STATE), F32)
            for lap in range(nz):
                z = nz - 1 - lap if u.scan else lap
                prefix[u.index, z, : u.share, :] = state
                products[u.index, z] = jnp.broadcast_to(product, (8, STATE))
                factor = decay_in[z, head, :]
                state = factor * state + scan_in[u.index, z, : u.share, :]
                product = product * factor
            total_send[u.index, : u.share, :] = state
            if nx > 1:
                ex_total(u).start_all()

    def scan_turn(u):
        @pl.when(my_half == u.half)
        def _():
            head = pl.ds((u.first + mz // 2 * u.share) // WIDTH, 1)
            state = jnp.zeros((u.share, STATE), F32)
            if nx > 1:
                total_in[u.index, mx, : u.share, :] = total_send[u.index, : u.share, :]
                ex_total(u).arrived()
                for lap in range(nx):
                    x = nx - 1 - lap if u.scan else lap
                    before = x > mx if u.scan else x < mx
                    moved = line_in[x, head, :] * state + total_in[u.index, x, : u.share, :]
                    state = jnp.where(before, moved, state)

            def turn(z):
                turned[u.index, z, : u.share, :] = (
                    prefix[u.index, z, : u.share, :] + products[u.index, z, :1, :] * state
                )

            def turn_to(z):
                turn(z)
                from_scanner(u).start(z)

            each(nz, mz, turn_to)
            turn(mz)
            ends[u.scan, my_rows(u), :] = turned[u.index, mz, : u.share, :]

    def scan_arrived(u):
        by_half(u.half, from_scanner(u).arrived)

    def scan_sent(u):
        by_half(u.half, to_scanner(u).sent)

        @pl.when(my_half == u.half)
        def _():
            ex_total(u).sent()
            from_scanner(u).sent()

    def send_grad(u):
        cols = u.cut()
        ex_dy[u.half].arrived()
        send_local(u, tn(grow[:, cols] * dyg[:, cols], cg[...]))

    def send_state(u):
        cols = u.cut()
        ex_x[u.index - 2].arrived()
        send_local(u, tn(wide_weight[:, cols] * wide_step[:, cols] * xg[:, cols], bg[...]))

    def send_dx(u):
        scan_arrived(u)
        cols = u.cut()
        whole = summed[:, cols] + wide_weight[:, cols] * nt(bg[...], ends[1, cols, :])
        summed[:, cols] = whole
        dx_buf[:, cols] = wide_step[:, cols] * whole + skip[:, cols] * dyg[:, cols]
        ex_dx[u.half].start_all()

    own_dy.wait()
    send_grad(grads_a)
    score_top[...] = nt(bg[:low, :], cg[...])
    score_low[...] = nt(bg[low:, :], cg[low:, :])
    lax.fori_loop(0, pairs, fill_decays, 0)

    def fill_summed(pair, carry):
        cols = pair_cols(pair)
        grads = dyg[:, cols]
        heads_of = (2 * pair, 2 * pair + 1)
        above = nn(
            jnp.concatenate([score_top[...] * decay_top[h] for h in heads_of], axis=0), grads
        )
        below = nn(
            jnp.concatenate([score_low[...] * decay_low[h] for h in heads_of], axis=0),
            grads[low:, :],
        )
        summed[:low, cols] = jnp.where(left_lanes[:low, :], above[:low, :], above[low:, :])
        summed[low:, cols] = jnp.where(left_lanes[:low, :], below[:low, :], below[low:, :])
        return carry

    def fill_grad_score(pair, carry):
        cols = pair_cols(pair)
        grads = dyg[:, cols]
        scaled = wide_step[:, cols] * xg[:, cols]
        sides = [jnp.where(left_lanes == (side == 0), scaled, 0.0) for side in range(2)]
        above = nt(jnp.concatenate([one[:low, :] for one in sides], axis=0), grads)
        below = nt(jnp.concatenate([one[low:, :] for one in sides], axis=0), grads[low:, :])
        mixed_top, mixed_low = [], []
        for side in range(2):
            h = 2 * pair + side
            mixed_top.append(above[side * low : (side + 1) * low, :] * decay_top[h])
            mixed_low.append(below[side * low : (side + 1) * low, :] * decay_low[h])
            sums = jnp.sum(mixed_top[side] * score_top[...], axis=0, keepdims=True)
            more = jnp.sum(mixed_low[side] * score_low[...], axis=0, keepdims=True)
            mine = lax.broadcasted_iota(jnp.int32, (hl, low), 0) == h
            row_sums[:, :low] += jnp.where(mine, sums[:, :low], 0.0)
            row_sums[:, low:] += jnp.where(mine, sums[:, low:] + more, 0.0)
        grad_top[...] += mixed_top[0] + mixed_top[1]
        grad_low[...] += mixed_low[0] + mixed_low[1]
        return carry

    grad_top[...] = jnp.zeros_like(grad_top)
    grad_low[...] = jnp.zeros_like(grad_low)
    row_sums[...] = jnp.zeros_like(row_sums)
    line_decays()
    send_grad(grads_b)
    lax.fori_loop(0, pairs // 2, fill_summed, 0)
    scan_line(grads_a)
    own_x.wait()
    send_state(states_a)
    scan_turn(grads_a)
    scan_line(grads_b)
    send_state(states_b)
    send_state(states_c)
    lax.fori_loop(pairs // 2, pairs, fill_summed, 0)
    scan_turn(grads_b)
    scan_line(states_a)
    send_dx(grads_a)
    scan_turn(states_a)
    scan_line(states_b)
    scan_line(states_c)
    lax.fori_loop(0, pairs - 1, fill_grad_score, 0)
    scan_turn(states_b)
    scan_turn(states_c)
    send_dx(grads_b)
    lax.fori_loop(pairs - 1, pairs, fill_grad_score, 0)
    end = ends[1]
    along = sum_nt(spread, xg[...] * summed[...])

    def by_target_core(half, stride, first, value):
        size = value.shape[0] // nh
        for target in range(nh):
            base = (target // 2) * stride + first
            half[target % 2, base : base + size, :] = value[target * size : (target + 1) * size, :]

    from_states = nn(wide_weight[...] * wide_step[...] * xg[...], end)
    by_target_core(db_half, tok, 0, from_states + jnp.concatenate(
        [nn(grad_top[...], cg[...]), nn(grad_low[...], cg[low:, :])], axis=0
    ))
    pair_db.start(sibling)
    from_score = jnp.concatenate(
        [
            tn(grad_top[:, :low], bg[:low, :]),
            tn(grad_top[:, low:], bg[:low, :]) + tn(grad_low[...], bg[low:, :]),
        ],
        axis=0,
    )
    outer = grow[...] * dyg[...]
    made = jnp.sum((end * locals_ref[0]).reshape(hl, WIDTH, STATE), axis=1)
    read_part = from_score
    along_read = row_sums[...] - step * along
    kept = []
    for u in (states_a, states_b, states_c):
        scan_arrived(u)
        start = ends[0, u.cut(), :]
        kept.append(
            jnp.sum((end[u.cut(), :] * start).reshape(u.count // WIDTH, WIDTH, STATE), axis=1)
        )
        read_part = read_part + nn(outer[:, u.cut()], start)
        along_read = along_read + sum_nt(
            spread[:, u.cut()], outer[:, u.cut()] * nt(cg[...], start)
        )
    by_target_core(dc_half, tail_rows, 0, read_part)
    kept = jnp.concatenate(kept, axis=0)
    last = jnp.sum(tail * kept + made, axis=1, keepdims=True)
    lane_t = lax.broadcasted_iota(jnp.int32, (hl, total), 1)
    grad_cum = along_read + jnp.where(lane_t == total - 1, last, 0.0)
    grad_log = exact_nn(grad_cum, (row_at >= col_at).astype(F32))
    grad_step = along - rate * grad_log
    for begin in range(0, total, heads):
        piece = grad_step[:, begin : min(total, begin + heads)]
        if piece.shape[1] < heads:
            piece = jnp.concatenate(
                [piece, jnp.zeros((hl, heads - piece.shape[1]), F32)], axis=1
            )
        turns = [pltpu.roll(piece, tok * t, 1) if t else piece for t in range(per_tile)]
        for spot in range(min(per_tile, nh)):
            target = begin // tok + spot
            placed = [turns[(c - spot) % per_tile] for c in range(2)]
            base = (target // 2) * tail_rows + tok
            dc_half[target % 2, base : base + hl, :heads] = jnp.where(
                lane_h == core, jnp.where(core == 0, placed[0], placed[1]), 0.0
            )
    pair_dc.start(sibling)
    pair_db.arrived()
    db_sum[...] = db_half[core] + db_got[...]
    ex_db.start_all()
    db_in[rows(my, tok), :] = db_sum[rows(my, tok), :]
    pair_dc.arrived()
    dc_sum[...] = dc_half[core] + dc_got[...]
    ex_dc.start_all()
    dc_in[rows(my, tail_rows), :] = dc_sum[rows(my, tail_rows), :]

    share = nc // groups

    def fold(received, stride, out):
        for g in range(groups):
            part = received[g * share * stride : g * share * stride + tok, :]
            for s in range(g * share + 1, (g + 1) * share):
                part = part + received[s * stride : s * stride + tok, :]
            out[:, g * STATE : (g + 1) * STATE] = part

    dx_ref[:, rows(me, width)] = dx_buf[rows(me, tok), :]
    for exchange in (*ex_dy, *ex_x, *ex_dx, relay, ex_decay, ex_line_decay):
        exchange.sent()
    packs_sent()
    for u in (grads_a, grads_b, states_a, states_b, states_c):
        scan_sent(u)
    for exchange in (pair_pack, pair_db, pair_dc):
        exchange.sent()
    for exchange in ex_dx:
        exchange.arrived()
    put_dx = pltpu.make_async_copy(dx_ref, dx_hbm, own_sems.at[2])
    put_dx.start()
    ex_db.arrived()
    fold(db_in, tok, dwrite_ref)
    ex_db.sent()
    ex_dc.arrived()
    fold(dc_in, tail_rows, dread_ref)
    by_heads = []
    for chip in range(nc):
        piece = dc_in[chip * tail_rows + tok : (chip + 1) * tail_rows, :heads]
        by_heads += [piece, pltpu.roll(piece, heads - tok, 1)]
    dstep_ref[...] = jnp.transpose(jnp.concatenate(by_heads, axis=0))[:tok, :]
    ex_dc.sent()
    put_dx.wait()


def hand_out(parts, *refs):
    count = len(parts)
    sems = refs[-1]
    copies = []
    for i in range(count):
        wide = refs[i].shape[1] // parts[i]
        for p in range(parts[i]):
            cols = slice(p * wide, (p + 1) * wide)
            through = refs[2 * count + i].at[:, cols]
            at = len(copies)
            copies.append(
                (
                    pltpu.make_async_copy(refs[i].at[:, cols], through, sems.at[0, at]),
                    pltpu.make_async_copy(through, refs[count + i].at[:, cols], sems.at[1, at]),
                )
            )
    for fetch, _ in copies:
        fetch.start()
    for fetch, put in copies:
        fetch.wait()
        put.start()
    for _, put in copies:
        put.wait()


def on_device(groups, features, write_proj, read_proj, step_size, decay_rate, skip_weight, upstream):
    nh = lax.axis_size("head")
    tok, heads = step_size.shape
    hl = heads // nh
    nz = hl
    nx = lax.axis_size("ctx") // nz
    width = hl * WIDTH
    nc = nh // 2
    total = nh * tok
    low = total // 2
    vmem = pl.BlockSpec(memory_space=pltpu.VMEM)
    hbm = pl.BlockSpec(memory_space=pltpu.HBM)

    def buf(*shape):
        return pltpu.VMEM(shape, F32)

    results = pl.pallas_call(
        functools.partial(kernel, nh, nx, nz, groups),
        out_shape=(
            jax.ShapeDtypeStruct(features.shape, F32),
            jax.ShapeDtypeStruct(write_proj.shape, F32),
            jax.ShapeDtypeStruct(read_proj.shape, F32),
            jax.ShapeDtypeStruct(step_size.shape, F32),
        ),
        in_specs=[hbm] * 7,
        out_specs=(hbm, vmem, vmem, vmem),
        scratch_shapes=[
            pltpu.SMEM(decay_rate.shape, F32),
            pltpu.SMEM(skip_weight.shape, F32),
            buf(*write_proj.shape),
            buf(*read_proj.shape),
            buf(*step_size.shape),
            buf(total, width),
            buf(total, width),
            buf(total, STATE),
            buf(total, STATE),
            buf(nc, 2 * tok + hl, STATE),
            buf(nh, 2 * tok + hl, STATE),
            buf(hl, total),
            buf(total, width),
            buf(total, width),
            buf(total, width),
            buf(total, width),
            buf(hl, low, total),
            buf(hl, low, low),
            buf(low, total),
            buf(low, low),
            buf(low, total),
            buf(low, low),
            buf(hl, total),
            buf(total, width),
            buf(total, width),
            buf(*features.shape),
            buf(2, hl * WIDTH, STATE),
            buf(5, nz, WIDTH, STATE),
            buf(5, WIDTH, STATE),
            buf(5, nx, WIDTH, STATE),
            buf(5, nz, WIDTH, STATE),
            buf(5, nz, 8, STATE),
            buf(5, nz, WIDTH, STATE),
            buf(2, hl * WIDTH, STATE),
            buf(hl, STATE),
            buf(nz, hl, STATE),
            buf(hl, STATE),
            buf(nx, hl, STATE),
            buf(2, nc * tok, STATE),
            buf(nc * tok, STATE),
            buf(nc * tok, STATE),
            buf(nc * tok, STATE),
            buf(2, nc * (tok + hl), STATE),
            buf(nc * (tok + hl), STATE),
            buf(nc * (tok + hl), STATE),
            buf(nc * (tok + hl), STATE),
            pltpu.SemaphoreType.DMA((30, 2)),
            pltpu.SemaphoreType.DMA((1 + nc,)),
            pltpu.SemaphoreType.DMA((8,)),
        ],
        compiler_params=pltpu.CompilerParams(
            collective_id=0, has_side_effects=True, vmem_limit_bytes=64 * 1024 * 1024
        ),
        cost_estimate=pl.CostEstimate(
            flops=1_200_000_000, bytes_accessed=8_000_000, transcendentals=600_000
        ),
    )(decay_rate, skip_weight, features, upstream, write_proj, read_proj, step_size)
    parts = (4, 1, 1, 1)
    return pl.pallas_call(
        functools.partial(hand_out, parts),
        out_shape=tuple(jax.ShapeDtypeStruct(r.shape, F32) for r in results),
        in_specs=[hbm] * len(results),
        out_specs=(hbm,) * len(results),
        scratch_shapes=[
            *(buf(*r.shape) for r in results),
            pltpu.SemaphoreType.DMA((2, sum(parts))),
        ],
        compiler_params=pltpu.CompilerParams(vmem_limit_bytes=64 * 1024 * 1024),
        cost_estimate=pl.CostEstimate(flops=0, bytes_accessed=1_200_000, transcendentals=0),
    )(*results)


def solution(mesh):
    tokens = P(("ctx", "head"), None)
    return jax.shard_map(
        functools.partial(on_device, GROUPS),
        mesh=mesh,
        in_specs=(tokens, tokens, tokens, tokens, P("head"), P("head"), tokens),
        out_specs=(tokens, tokens, tokens, tokens),
        check_vma=False,
    )
```

```python
import functools

import jax
import jax.numpy as jnp
from jax import lax
from jax.experimental import pallas as pl
from jax.experimental.pallas import tpu as pltpu
from jax.sharding import PartitionSpec as P

STATE = 128
GROUPS = 4
WIDTH = 64
MESH = pl.DeviceIdType.MESH
F32 = jnp.float32
HIGH = lax.Precision.HIGH


def mm(a, b, dims, precision=HIGH):
    return lax.dot_general(
        a, b, (dims, ((), ())), precision=precision, preferred_element_type=F32
    )


def nn(a, b, precision=HIGH):
    return mm(a, b, ((1,), (0,)), precision)


def nt(a, b, precision=HIGH):
    return mm(a, b, ((1,), (1,)), precision)


def tn(a, b, precision=HIGH):
    return mm(a, b, ((0,), (0,)), precision)


def parts_of(a, count):
    out = []
    for _ in range(count):
        piece = a.astype(jnp.bfloat16)
        out.append(piece)
        a = a - piece.astype(F32)
    return out


def exact_nn(a, ones):
    n = a.shape[0]
    stacked = jnp.concatenate([p.astype(F32) for p in parts_of(a, 3)], axis=0)
    out = nn(stacked.astype(jnp.bfloat16), ones.astype(jnp.bfloat16), None)
    return (out[2 * n :] + out[n : 2 * n]) + out[:n]


def exact_tn(a, ones):
    stacked = jnp.concatenate([p.astype(F32) for p in parts_of(a, 3)][::-1], axis=0)
    tall = jnp.concatenate([ones] * 3, axis=0)
    return tn(stacked.astype(jnp.bfloat16), tall.astype(jnp.bfloat16), None)


def sum_nt(ones, b):
    ones = ones.astype(jnp.bfloat16)
    first, second = parts_of(b, 2)
    return nt(ones, second, None) + nt(ones, first, None)


class Unit:
    def __init__(self, index, scan, half, first, count, scanners):
        self.index, self.scan, self.half = index, scan, half
        self.first, self.count, self.share = first, count, count // scanners

    def cut(self):
        return slice(self.first, self.first + self.count)


class Exchange:
    def __init__(self, count, me, device, src, dst, sems, bulk):
        self.count, self.me, self.device = count, me, device
        self.src, self.dst, self.sems, self.bulk = src, dst, sems, bulk

    def start(self, to):
        pltpu.make_async_remote_copy(
            src_ref=self.src(to),
            dst_ref=self.dst(self.me),
            send_sem=self.sems.at[0],
            recv_sem=self.sems.at[1],
            device_id=self.device(to),
            device_id_type=MESH,
        ).start()

    def start_all(self):
        each(self.count, self.me, self.start)

    def whole(self, blocks):
        return pltpu.make_async_remote_copy(
            src_ref=self.bulk(blocks),
            dst_ref=self.bulk(blocks),
            send_sem=self.sems.at[0],
            recv_sem=self.sems.at[1],
            device_id=self.device(lax.rem(self.me + 1, self.count)),
            device_id_type=MESH,
        )

    def arrived(self, blocks=None):
        if self.count > 1:
            self.whole(blocks or self.count - 1).wait_recv()

    def sent(self, blocks=None):
        if self.count > 1:
            self.whole(blocks or self.count - 1).wait_send()


def each(count, me, act):
    if count % 2 == 0:
        act(lax.rem(me + count // 2, count))
    for j in range((count - 1) // 2, 0, -1):
        act(lax.rem(me + j, count))
        act(lax.rem(me + count - j, count))


def rows(index, size):
    return pl.ds(pl.multiple_of(index * size, size), size)


def kernel(
    nh, nx, nz, groups,
    rate_hbm, skip_hbm, x_hbm, dy_hbm, write_hbm, read_hbm, step_hbm,
    dx_ref, dwrite_ref, dread_ref, dstep_ref,
    rate_ref, skip_ref, write_ref, read_ref, step_ref,
    xg, dyg, bg, cg, pack_out, pack_in,
    cum_ref, wide_cum, grow, wide_step, wide_weight,
    decay_top, decay_low, score_top, score_low, grad_top, grad_low, row_sums,
    summed, dx_buf,
    locals_ref, scan_in, total_send, total_in, prefix, products, turned, ends,
    decay_out, decay_in, line_out, line_in,
    db_half, db_got, db_sum, db_in, dc_half, dc_got, dc_sum, dc_in,
    sems, pack_sems, own_sems,
):
    tok = step_ref.shape[0]
    heads = step_ref.shape[1]
    hl = heads // nh
    nc = nh // 2
    width = hl * WIDTH
    total = nh * tok
    low = total // 2
    pairs = hl // 2
    hh = hl // 2
    part = hh * WIDTH
    tail_rows = tok + hl
    me = lax.axis_index("head")
    at = lax.axis_index("ctx")
    my = me // 2
    core = lax.rem(me, 2)
    sibling = 1 - core
    mx = at // nz
    mz = lax.rem(at, nz)
    of_group = heads // groups

    def by_head(other):
        return {"head": other}

    def by_chip(other):
        return {"head": other * 2 + core}

    def by_core(other):
        return {"head": my * 2 + other}

    def by_z(other):
        return {"ctx": mx * nz + other}

    def by_x(other):
        return {"ctx": other * nz + mz}

    barrier = pltpu.get_barrier_semaphore()

    fetches = [
        pltpu.make_async_copy(src, dst, own_sems.at[3 + i])
        for i, (src, dst) in enumerate(
            (
                (step_hbm, step_ref),
                (write_hbm, write_ref),
                (read_hbm, read_ref),
                (rate_hbm, rate_ref),
                (skip_hbm, skip_ref),
            )
        )
    ]

    def greet(device):
        return lambda other: pl.semaphore_signal(
            barrier, inc=1, device_id=device(other), device_id_type=MESH
        )

    each(nh, me, greet(by_head))
    each(nz, mz, greet(by_z))
    if nx > 1:
        each(nx, mx, greet(by_x))
    for fetch in fetches:
        fetch.start()

    def columns(ref):
        return lambda other: ref.at[:, rows(other, width)]

    def some_columns(ref, first, size):
        return lambda other: ref.at[
            :, pl.ds(pl.multiple_of(other * width + first, size), size)
        ]

    def some_block(ref, first, size):
        return lambda other: ref.at[rows(other, tok), first : first + size]

    def block(ref, size):
        return lambda other: ref.at[rows(other, size), :]

    def along_head(src, dst, which, bulk):
        return Exchange(nh, me, by_head, src, dst, sems.at[which], bulk)

    def along_chip(src, dst, which, bulk):
        return Exchange(nc, my, by_chip, src, dst, sems.at[which], bulk)

    def across_core(src, dst, which, bulk):
        return Exchange(2, core, by_core, src, dst, sems.at[which], bulk)

    def first_rows(ref, size, cut=(0, None)):
        if cut[1] is None:
            return lambda n: ref.at[: n * size, :]
        return lambda n: ref.at[: n * size, cut[0] : cut[0] + cut[1]]

    halves = ((0, part), (part, part))
    ex_dy = [
        along_head(
            some_columns(dy_hbm, *cut), some_block(dyg, *cut), i, first_rows(dyg, tok, cut)
        )
        for i, cut in enumerate(halves)
    ]
    ex_dx = [
        along_head(
            some_block(dx_buf, *cut), some_columns(dx_ref, *cut), 2 + i,
            first_rows(dx_buf, tok, cut),
        )
        for i, cut in enumerate(halves)
    ]
    ex_x = [
        along_head(
            some_columns(x_hbm, *cut), some_block(xg, *cut), 4 + i, first_rows(xg, tok, cut)
        )
        for i, cut in enumerate(
            ((0, part), (part, part // 2), (part + part // 2, part // 2))
        )
    ]
    ex_db = along_chip(block(db_sum, tok), block(db_in, tok), 7, first_rows(db_in, tok))
    ex_dc = along_chip(
        block(dc_sum, tail_rows), block(dc_in, tail_rows), 8, first_rows(dc_in, tail_rows)
    )
    pair_pack = across_core(
        lambda t: pack_out.at[my], lambda s: pack_in.at[2 * my + s], 9, lambda n: pack_in.at[0]
    )
    pair_db = across_core(lambda t: db_half.at[t], lambda s: db_got, 10, lambda n: db_got)
    pair_dc = across_core(lambda t: dc_half.at[t], lambda s: dc_got, 11, lambda n: dc_got)
    relay = Exchange(
        nc, my, lambda t: by_core(sibling),
        lambda s: pack_in.at[2 * s + core], lambda s: None, sems.at[12],
        lambda n: pack_in.at[:n],
    )

    def pack_copy(to, slot):
        return pltpu.make_async_remote_copy(
            src_ref=pack_out.at[to],
            dst_ref=pack_in.at[2 * slot + core],
            send_sem=pack_sems.at[0],
            recv_sem=pack_sems.at[1 + slot],
            device_id=by_chip(to),
            device_id_type=MESH,
        )

    def packs_sent():
        if nc > 1:
            pltpu.make_async_remote_copy(
                src_ref=pack_out.at[: nc - 1],
                dst_ref=pack_out.at[: nc - 1],
                send_sem=pack_sems.at[0],
                recv_sem=pack_sems.at[1],
                device_id=by_chip(my),
                device_id_type=MESH,
            ).wait_send()

    grads_a = Unit(0, 1, 0, 0, part, hh)
    grads_b = Unit(1, 1, 1, part, part, hh)
    states_a = Unit(2, 0, 0, 0, part, hh)
    states_b = Unit(3, 0, 1, part, part // 2, hh)
    states_c = Unit(4, 0, 1, part + part // 2, part // 2, hh)
    my_half = lax.rem(mz, 2)

    def rows_of(u, i):
        return pl.ds(pl.multiple_of(u.first + i * u.share, u.share), u.share)

    def my_rows(u):
        return rows_of(u, mz // 2)

    def to_scanner(u):
        return Exchange(
            nz, mz, by_z,
            lambda t: locals_ref.at[u.scan, rows_of(u, t // 2), :],
            lambda s: scan_in.at[u.index, s, : u.share, :],
            sems.at[13 + u.index],
            lambda n: scan_in.at[u.index, :n, : u.share, :],
        )

    def from_scanner(u):
        return Exchange(
            nz, mz, by_z,
            lambda t: turned.at[u.index, t, : u.share, :],
            lambda s: ends.at[u.scan, my_rows(u), :],
            sems.at[18 + u.index],
            lambda n: turned.at[u.index, :n, : u.share, :],
        )

    def ex_total(u):
        return Exchange(
            nx, mx, by_x,
            lambda t: total_send.at[u.index, : u.share, :],
            lambda s: total_in.at[u.index, s, : u.share, :],
            sems.at[23 + u.index],
            lambda n: total_in.at[u.index, :n, : u.share, :],
        )

    ex_decay = Exchange(
        nz, mz, by_z, lambda t: decay_out, lambda s: decay_in.at[s], sems.at[28],
        lambda n: decay_in.at[:n],
    )
    ex_line_decay = Exchange(
        nx, mx, by_x, lambda t: line_out, lambda s: line_in.at[s], sems.at[29],
        lambda n: line_in.at[:n],
    )

    def by_half(half, act):
        @pl.when(my_half == half)
        def _():
            if hh > 1:
                act(hh - 1)

        @pl.when(my_half != half)
        def _():
            act(hh)

    def scanners(half, act):
        for j in range(hh):
            i = lax.rem(mz // 2 + hh // 2 + j, hh)

            @pl.when(2 * i + half != mz)
            def _(z=2 * i + half):
                act(z)

    own_dy = pltpu.make_async_copy(columns(dy_hbm)(me), block(dyg, tok)(me), own_sems.at[0])
    own_x = pltpu.make_async_copy(columns(x_hbm)(me), block(xg, tok)(me), own_sems.at[1])
    own_dy.start()
    own_x.start()
    for fetch in fetches:
        fetch.wait()
    padded = jnp.concatenate([step_ref[...], jnp.zeros((heads - tok, heads), F32)], axis=0)
    flipped = jnp.transpose(padded)
    for target in range(nc):
        g = target * 2 * hl // of_group
        pack_out[target, :tok, :] = write_ref[:, g * STATE : (g + 1) * STATE]
        pack_out[target, tok : 2 * tok, :] = read_ref[:, g * STATE : (g + 1) * STATE]
        first = target * 2 * hl
        pack_out[target, 2 * tok :, :heads] = flipped[first : first + hl, :] + pltpu.roll(
            flipped[first + hl : first + 2 * hl, :], tok, 1
        )
    pack_in[me] = pack_out[my]

    pl.semaphore_wait(barrier, (nh - 1) + (nz - 1) + (nx - 1))

    pair_pack.start(sibling)
    each(nc, my, lambda to: pack_copy(to, my).start())
    for exchange in ex_dy:
        exchange.start_all()

    def hand_on(chip):
        pack_copy(chip, chip).wait_recv()
        pltpu.make_async_remote_copy(
            src_ref=pack_in.at[2 * chip + core],
            dst_ref=pack_in.at[2 * chip + core],
            send_sem=sems.at[12, 0],
            recv_sem=sems.at[12, 1],
            device_id=by_core(sibling),
            device_id_type=MESH,
        ).start()

    each(nc, my, hand_on)
    for exchange in ex_x:
        exchange.start_all()
    pair_pack.arrived()
    relay.arrived()
    bg[...] = pack_in[:, :tok, :].reshape(total, STATE)
    cg[...] = pack_in[:, tok : 2 * tok, :].reshape(total, STATE)

    per_tile = heads // tok
    lane_h = lax.broadcasted_iota(jnp.int32, (hl, heads), 1) // tok
    tiles = []
    for first_source in range(0, nh, per_tile):
        tile = jnp.zeros((hl, heads), F32)
        for source in range(first_source, min(nh, first_source + per_tile)):
            spot = source - first_source
            piece = pack_in[source, 2 * tok :, :heads]
            both = []
            for c in range(2):
                shift = (heads + tok * (spot - c)) % heads
                both.append(pltpu.roll(piece, shift, 1) if shift else piece)
            tile = jnp.where(lane_h == spot, jnp.where(core == 0, both[0], both[1]), tile)
        tiles.append(tile)
    step = jnp.concatenate(tiles, axis=1)[:, :total]
    place = lax.broadcasted_iota(jnp.int32, (hl, 1), 0)
    rate = jnp.zeros((hl, 1), F32)
    for h in range(hl):
        rate = jnp.where(place == h, rate_ref[h], rate)
    lane = lax.broadcasted_iota(jnp.int32, (1, width), 1)
    skip = jnp.zeros((1, width), F32)
    for h in range(hl):
        skip = jnp.where(lane // WIDTH == h, skip_ref[h], skip)
    row_at = lax.broadcasted_iota(jnp.int32, (total, total), 0)
    col_at = lax.broadcasted_iota(jnp.int32, (total, total), 1)
    cumul = exact_nn(-step * rate, (col_at >= row_at).astype(F32))
    cum_ref[...] = cumul
    tail = jnp.exp(cumul[:, total - 1 : total])
    spread = (
        lax.broadcasted_iota(jnp.int32, (hl, width), 1) // WIDTH
        == lax.broadcasted_iota(jnp.int32, (hl, width), 0)
    ).astype(F32)
    wide = exact_tn(cumul, spread)
    wide_cum[...] = wide
    grow[...] = jnp.exp(wide)
    wide_weight[...] = jnp.exp(wide[total - 1 : total, :] - wide)
    wide_step[...] = exact_tn(step, spread)
    decay_out[...] = jnp.broadcast_to(tail, (hl, STATE))
    ex_decay.start_all()
    decay_in[mz] = decay_out[...]
    left_lanes = lax.broadcasted_iota(jnp.int32, (total, 2 * WIDTH), 1) < WIDTH
    later = lax.broadcasted_iota(jnp.int32, (low, low), 1) >= lax.broadcasted_iota(
        jnp.int32, (low, low), 0
    )

    def pair_cols(pair):
        return rows(pair, 2 * WIDTH)

    def masked(gap):
        return jnp.where(later, jnp.exp(jnp.where(later, gap, 0.0)), 0.0)

    def fill_decays(pair, carry):
        here = wide_cum[:, pair_cols(pair)]
        turned_round = pltpu.roll(here, WIDTH, 1)
        for side in range(2):
            h = 2 * pair + side
            col = jnp.where(left_lanes == (side == 0), here, turned_round)[:, :low]
            row = cum_ref[pl.ds(h, 1), :]
            decay_top[h, :, :low] = masked(row[:, :low] - col[:low, :])
            decay_top[h, :, low:] = jnp.exp(row[:, low:] - col[:low, :])
            decay_low[h] = masked(row[:, low:] - col[low:, :])
        return carry

    def send_local(u, local):
        locals_ref[u.scan, u.cut(), :] = local
        scanners(u.half, to_scanner(u).start)

        @pl.when(my_half == u.half)
        def _():
            scan_in[u.index, mz, : u.share, :] = locals_ref[u.scan, my_rows(u), :]

    def line_decays():
        ex_decay.arrived()
        product = decay_in[0]
        for z in range(1, nz):
            product = product * decay_in[z]
        line_out[...] = product
        line_in[mx] = product
        if nx > 1:
            ex_line_decay.start_all()
            ex_line_decay.arrived()

    def scan_line(u):
        @pl.when(my_half == u.half)
        def _():
            head = pl.ds((u.first + mz // 2 * u.share) // WIDTH, 1)
            to_scanner(u).arrived()
            state = jnp.zeros((u.share, STATE), F32)
            product = jnp.ones((1, STATE), F32)
            for lap in range(nz):
                z = nz - 1 - lap if u.scan else lap
                prefix[u.index, z, : u.share, :] = state
                products[u.index, z] = jnp.broadcast_to(product, (8, STATE))
                factor = decay_in[z, head, :]
                state = factor * state + scan_in[u.index, z, : u.share, :]
                product = product * factor
            total_send[u.index, : u.share, :] = state
            if nx > 1:
                ex_total(u).start_all()

    def scan_turn(u):
        @pl.when(my_half == u.half)
        def _():
            head = pl.ds((u.first + mz // 2 * u.share) // WIDTH, 1)
            state = jnp.zeros((u.share, STATE), F32)
            if nx > 1:
                total_in[u.index, mx, : u.share, :] = total_send[u.index, : u.share, :]
                ex_total(u).arrived()
                for lap in range(nx):
                    x = nx - 1 - lap if u.scan else lap
                    before = x > mx if u.scan else x < mx
                    moved = line_in[x, head, :] * state + total_in[u.index, x, : u.share, :]
                    state = jnp.where(before, moved, state)

            def turn(z):
                turned[u.index, z, : u.share, :] = (
                    prefix[u.index, z, : u.share, :] + products[u.index, z, :1, :] * state
                )

            def turn_to(z):
                turn(z)
                from_scanner(u).start(z)

            each(nz, mz, turn_to)
            turn(mz)
            ends[u.scan, my_rows(u), :] = turned[u.index, mz, : u.share, :]

    def scan_arrived(u):
        by_half(u.half, from_scanner(u).arrived)

    def scan_sent(u):
        by_half(u.half, to_scanner(u).sent)

        @pl.when(my_half == u.half)
        def _():
            ex_total(u).sent()
            from_scanner(u).sent()

    def send_grad(u):
        cols = u.cut()
        ex_dy[u.half].arrived()
        send_local(u, tn(grow[:, cols] * dyg[:, cols], cg[...]))

    def send_state(u):
        cols = u.cut()
        ex_x[u.index - 2].arrived()
        send_local(u, tn(wide_weight[:, cols] * wide_step[:, cols] * xg[:, cols], bg[...]))

    def send_dx(u):
        scan_arrived(u)
        cols = u.cut()
        whole = summed[:, cols] + wide_weight[:, cols] * nt(bg[...], ends[1, cols, :])
        summed[:, cols] = whole
        dx_buf[:, cols] = wide_step[:, cols] * whole + skip[:, cols] * dyg[:, cols]
        ex_dx[u.half].start_all()

    own_dy.wait()
    send_grad(grads_a)
    score_top[...] = nt(bg[:low, :], cg[...])
    score_low[...] = nt(bg[low:, :], cg[low:, :])
    lax.fori_loop(0, pairs, fill_decays, 0)

    def fill_summed(pair, carry):
        cols = pair_cols(pair)
        grads = dyg[:, cols]
        heads_of = (2 * pair, 2 * pair + 1)
        above = nn(
            jnp.concatenate([score_top[...] * decay_top[h] for h in heads_of], axis=0), grads
        )
        below = nn(
            jnp.concatenate([score_low[...] * decay_low[h] for h in heads_of], axis=0),
            grads[low:, :],
        )
        summed[:low, cols] = jnp.where(left_lanes[:low, :], above[:low, :], above[low:, :])
        summed[low:, cols] = jnp.where(left_lanes[:low, :], below[:low, :], below[low:, :])
        return carry

    def fill_grad_score(pair, carry):
        cols = pair_cols(pair)
        grads = dyg[:, cols]
        scaled = wide_step[:, cols] * xg[:, cols]
        sides = [jnp.where(left_lanes == (side == 0), scaled, 0.0) for side in range(2)]
        above = nt(jnp.concatenate([one[:low, :] for one in sides], axis=0), grads)
        below = nt(jnp.concatenate([one[low:, :] for one in sides], axis=0), grads[low:, :])
        mixed_top, mixed_low = [], []
        for side in range(2):
            h = 2 * pair + side
            mixed_top.append(above[side * low : (side + 1) * low, :] * decay_top[h])
            mixed_low.append(below[side * low : (side + 1) * low, :] * decay_low[h])
            sums = jnp.sum(mixed_top[side] * score_top[...], axis=0, keepdims=True)
            more = jnp.sum(mixed_low[side] * score_low[...], axis=0, keepdims=True)
            mine = lax.broadcasted_iota(jnp.int32, (hl, low), 0) == h
            row_sums[:, :low] += jnp.where(mine, sums[:, :low], 0.0)
            row_sums[:, low:] += jnp.where(mine, sums[:, low:] + more, 0.0)
        grad_top[...] += mixed_top[0] + mixed_top[1]
        grad_low[...] += mixed_low[0] + mixed_low[1]
        return carry

    grad_top[...] = jnp.zeros_like(grad_top)
    grad_low[...] = jnp.zeros_like(grad_low)
    row_sums[...] = jnp.zeros_like(row_sums)
    line_decays()
    send_grad(grads_b)
    lax.fori_loop(0, pairs // 2, fill_summed, 0)
    scan_line(grads_a)
    own_x.wait()
    send_state(states_a)
    scan_turn(grads_a)
    scan_line(grads_b)
    send_state(states_b)
    send_state(states_c)
    lax.fori_loop(pairs // 2, pairs, fill_summed, 0)
    scan_turn(grads_b)
    scan_line(states_a)
    send_dx(grads_a)
    scan_turn(states_a)
    scan_line(states_b)
    scan_line(states_c)
    lax.fori_loop(0, pairs - 1, fill_grad_score, 0)
    scan_turn(states_b)
    scan_turn(states_c)
    send_dx(grads_b)
    lax.fori_loop(pairs - 1, pairs, fill_grad_score, 0)
    end = ends[1]
    along = sum_nt(spread, xg[...] * summed[...])

    def by_target_core(half, stride, first, value):
        size = value.shape[0] // nh
        for target in range(nh):
            base = (target // 2) * stride + first
            half[target % 2, base : base + size, :] = value[target * size : (target + 1) * size, :]

    from_states = nn(wide_weight[...] * wide_step[...] * xg[...], end)
    by_target_core(db_half, tok, 0, from_states + jnp.concatenate(
        [nn(grad_top[...], cg[...]), nn(grad_low[...], cg[low:, :])], axis=0
    ))
    pair_db.start(sibling)
    from_score = jnp.concatenate(
        [
            tn(grad_top[:, :low], bg[:low, :]),
            tn(grad_top[:, low:], bg[:low, :]) + tn(grad_low[...], bg[low:, :]),
        ],
        axis=0,
    )
    outer = grow[...] * dyg[...]
    made = jnp.sum((end * locals_ref[0]).reshape(hl, WIDTH, STATE), axis=1)
    read_part = from_score
    along_read = row_sums[...] - step * along
    kept = []
    for u in (states_a, states_b, states_c):
        scan_arrived(u)
        start = ends[0, u.cut(), :]
        kept.append(
            jnp.sum((end[u.cut(), :] * start).reshape(u.count // WIDTH, WIDTH, STATE), axis=1)
        )
        read_part = read_part + nn(outer[:, u.cut()], start)
        along_read = along_read + sum_nt(
            spread[:, u.cut()], outer[:, u.cut()] * nt(cg[...], start)
        )
    by_target_core(dc_half, tail_rows, 0, read_part)
    kept = jnp.concatenate(kept, axis=0)
    last = jnp.sum(tail * kept + made, axis=1, keepdims=True)
    lane_t = lax.broadcasted_iota(jnp.int32, (hl, total), 1)
    grad_cum = along_read + jnp.where(lane_t == total - 1, last, 0.0)
    grad_log = exact_nn(grad_cum, (row_at >= col_at).astype(F32))
    grad_step = along - rate * grad_log
    for begin in range(0, total, heads):
        piece = grad_step[:, begin : min(total, begin + heads)]
        if piece.shape[1] < heads:
            piece = jnp.concatenate(
                [piece, jnp.zeros((hl, heads - piece.shape[1]), F32)], axis=1
            )
        turns = [pltpu.roll(piece, tok * t, 1) if t else piece for t in range(per_tile)]
        for spot in range(min(per_tile, nh)):
            target = begin // tok + spot
            placed = [turns[(c - spot) % per_tile] for c in range(2)]
            base = (target // 2) * tail_rows + tok
            dc_half[target % 2, base : base + hl, :heads] = jnp.where(
                lane_h == core, jnp.where(core == 0, placed[0], placed[1]), 0.0
            )
    pair_dc.start(sibling)
    pair_db.arrived()
    db_sum[...] = db_half[core] + db_got[...]
    ex_db.start_all()
    db_in[rows(my, tok), :] = db_sum[rows(my, tok), :]
    pair_dc.arrived()
    dc_sum[...] = dc_half[core] + dc_got[...]
    ex_dc.start_all()
    dc_in[rows(my, tail_rows), :] = dc_sum[rows(my, tail_rows), :]

    share = nc // groups

    def fold(received, stride, out):
        for g in range(groups):
            part = received[g * share * stride : g * share * stride + tok, :]
            for s in range(g * share + 1, (g + 1) * share):
                part = part + received[s * stride : s * stride + tok, :]
            out[:, g * STATE : (g + 1) * STATE] = part

    own_dx = pltpu.make_async_copy(block(dx_buf, tok)(me), columns(dx_ref)(me), own_sems.at[2])
    own_dx.start()
    for exchange in (*ex_dy, *ex_x, *ex_dx, relay, ex_decay, ex_line_decay):
        exchange.sent()
    packs_sent()
    for u in (grads_a, grads_b, states_a, states_b, states_c):
        scan_sent(u)
    for exchange in (pair_pack, pair_db, pair_dc):
        exchange.sent()
    for exchange in ex_dx:
        exchange.arrived()
    ex_db.arrived()
    fold(db_in, tok, dwrite_ref)
    ex_db.sent()
    ex_dc.arrived()
    fold(dc_in, tail_rows, dread_ref)
    by_heads = []
    for chip in range(nc):
        piece = dc_in[chip * tail_rows + tok : (chip + 1) * tail_rows, :heads]
        by_heads += [piece, pltpu.roll(piece, heads - tok, 1)]
    dstep_ref[...] = jnp.transpose(jnp.concatenate(by_heads, axis=0))[:tok, :]
    ex_dc.sent()
    own_dx.wait()


def hand_out(parts, *refs):
    count = len(parts)
    sems = refs[-1]
    copies = []
    for i in range(count):
        wide = refs[i].shape[1] // parts[i]
        for p in range(parts[i]):
            cols = slice(p * wide, (p + 1) * wide)
            copies.append(
                pltpu.make_async_copy(
                    refs[i].at[:, cols], refs[count + i].at[:, cols], sems.at[len(copies)]
                )
            )
    for copy in copies:
        copy.start()
    for copy in copies:
        copy.wait()


def on_device(groups, features, write_proj, read_proj, step_size, decay_rate, skip_weight, upstream):
    nh = lax.axis_size("head")
    tok, heads = step_size.shape
    hl = heads // nh
    nz = hl
    nx = lax.axis_size("ctx") // nz
    width = hl * WIDTH
    nc = nh // 2
    total = nh * tok
    low = total // 2
    vmem = pl.BlockSpec(memory_space=pltpu.VMEM)
    hbm = pl.BlockSpec(memory_space=pltpu.HBM)

    def buf(*shape):
        return pltpu.VMEM(shape, F32)

    results = pl.pallas_call(
        functools.partial(kernel, nh, nx, nz, groups),
        out_shape=(
            jax.ShapeDtypeStruct(features.shape, F32),
            jax.ShapeDtypeStruct(write_proj.shape, F32),
            jax.ShapeDtypeStruct(read_proj.shape, F32),
            jax.ShapeDtypeStruct(step_size.shape, F32),
        ),
        in_specs=[hbm] * 7,
        out_specs=(vmem, vmem, vmem, vmem),
        scratch_shapes=[
            pltpu.SMEM(decay_rate.shape, F32),
            pltpu.SMEM(skip_weight.shape, F32),
            buf(*write_proj.shape),
            buf(*read_proj.shape),
            buf(*step_size.shape),
            buf(total, width),
            buf(total, width),
            buf(total, STATE),
            buf(total, STATE),
            buf(nc, 2 * tok + hl, STATE),
            buf(nh, 2 * tok + hl, STATE),
            buf(hl, total),
            buf(total, width),
            buf(total, width),
            buf(total, width),
            buf(total, width),
            buf(hl, low, total),
            buf(hl, low, low),
            buf(low, total),
            buf(low, low),
            buf(low, total),
            buf(low, low),
            buf(hl, total),
            buf(total, width),
            buf(total, width),
            buf(2, hl * WIDTH, STATE),
            buf(5, nz, WIDTH, STATE),
            buf(5, WIDTH, STATE),
            buf(5, nx, WIDTH, STATE),
            buf(5, nz, WIDTH, STATE),
            buf(5, nz, 8, STATE),
            buf(5, nz, WIDTH, STATE),
            buf(2, hl * WIDTH, STATE),
            buf(hl, STATE),
            buf(nz, hl, STATE),
            buf(hl, STATE),
            buf(nx, hl, STATE),
            buf(2, nc * tok, STATE),
            buf(nc * tok, STATE),
            buf(nc * tok, STATE),
            buf(nc * tok, STATE),
            buf(2, nc * (tok + hl), STATE),
            buf(nc * (tok + hl), STATE),
            buf(nc * (tok + hl), STATE),
            buf(nc * (tok + hl), STATE),
            pltpu.SemaphoreType.DMA((30, 2)),
            pltpu.SemaphoreType.DMA((1 + nc,)),
            pltpu.SemaphoreType.DMA((8,)),
        ],
        compiler_params=pltpu.CompilerParams(
            collective_id=0, has_side_effects=True, vmem_limit_bytes=40 * 1024 * 1024
        ),
        cost_estimate=pl.CostEstimate(
            flops=1_200_000_000, bytes_accessed=8_000_000, transcendentals=600_000
        ),
    )(
        *(
            pltpu.with_memory_space_constraint(a, pltpu.HBM)
            for a in (
                decay_rate, skip_weight, features, upstream, write_proj, read_proj, step_size
            )
        )
    )
    parts = (4, 1, 1, 1)
    return pl.pallas_call(
        functools.partial(hand_out, parts),
        out_shape=tuple(jax.ShapeDtypeStruct(r.shape, F32) for r in results),
        in_specs=[vmem] * len(results),
        out_specs=(hbm,) * len(results),
        scratch_shapes=[pltpu.SemaphoreType.DMA((sum(parts),))],
        compiler_params=pltpu.CompilerParams(vmem_limit_bytes=16 * 1024 * 1024),
        cost_estimate=pl.CostEstimate(flops=0, bytes_accessed=1_200_000, transcendentals=0),
    )(*(pltpu.with_memory_space_constraint(r, pltpu.VMEM) for r in results))


def solution(mesh):
    tokens = P(("ctx", "head"), None)
    return jax.shard_map(
        functools.partial(on_device, GROUPS),
        mesh=mesh,
        in_specs=(tokens, tokens, tokens, tokens, P("head"), P("head"), tokens),
        out_specs=(tokens, tokens, tokens, tokens),
        check_vma=False,
    )
```

```python
import functools

import jax
import jax.numpy as jnp
from jax import lax
from jax.experimental import pallas as pl
from jax.experimental.pallas import tpu as pltpu
from jax.sharding import PartitionSpec as P

STATE = 128
GROUPS = 4
WIDTH = 64
MESH = pl.DeviceIdType.MESH
F32 = jnp.float32
HIGH = lax.Precision.HIGH


def mm(a, b, dims, precision=HIGH):
    return lax.dot_general(
        a, b, (dims, ((), ())), precision=precision, preferred_element_type=F32
    )


def nn(a, b, precision=HIGH):
    return mm(a, b, ((1,), (0,)), precision)


def nt(a, b, precision=HIGH):
    return mm(a, b, ((1,), (1,)), precision)


def tn(a, b, precision=HIGH):
    return mm(a, b, ((0,), (0,)), precision)


def parts_of(a, count):
    out = []
    for _ in range(count):
        piece = a.astype(jnp.bfloat16)
        out.append(piece)
        a = a - piece.astype(F32)
    return out


def exact_nn(a, ones):
    n = a.shape[0]
    stacked = jnp.concatenate([p.astype(F32) for p in parts_of(a, 3)], axis=0)
    out = nn(stacked.astype(jnp.bfloat16), ones.astype(jnp.bfloat16), None)
    return (out[2 * n :] + out[n : 2 * n]) + out[:n]


def exact_tn(a, ones):
    stacked = jnp.concatenate([p.astype(F32) for p in parts_of(a, 3)][::-1], axis=0)
    tall = jnp.concatenate([ones] * 3, axis=0)
    return tn(stacked.astype(jnp.bfloat16), tall.astype(jnp.bfloat16), None)


def sum_nt(ones, b):
    ones = ones.astype(jnp.bfloat16)
    first, second = parts_of(b, 2)
    return nt(ones, second, None) + nt(ones, first, None)


class Unit:
    def __init__(self, index, scan, half, first, count, scanners):
        self.index, self.scan, self.half = index, scan, half
        self.first, self.count, self.share = first, count, count // scanners

    def cut(self):
        return slice(self.first, self.first + self.count)


class Exchange:
    def __init__(self, count, me, device, src, dst, sems, bulk):
        self.count, self.me, self.device = count, me, device
        self.src, self.dst, self.sems, self.bulk = src, dst, sems, bulk

    def start(self, to):
        pltpu.make_async_remote_copy(
            src_ref=self.src(to),
            dst_ref=self.dst(self.me),
            send_sem=self.sems.at[0],
            recv_sem=self.sems.at[1],
            device_id=self.device(to),
            device_id_type=MESH,
        ).start()

    def start_all(self):
        each(self.count, self.me, self.start)

    def whole(self, blocks):
        return pltpu.make_async_remote_copy(
            src_ref=self.bulk(blocks),
            dst_ref=self.bulk(blocks),
            send_sem=self.sems.at[0],
            recv_sem=self.sems.at[1],
            device_id=self.device(lax.rem(self.me + 1, self.count)),
            device_id_type=MESH,
        )

    def arrived(self, blocks=None):
        if self.count > 1:
            self.whole(blocks or self.count - 1).wait_recv()

    def sent(self, blocks=None):
        if self.count > 1:
            self.whole(blocks or self.count - 1).wait_send()


def others(count, me):
    out = [lax.rem(me + count // 2, count)] if count % 2 == 0 else []
    for j in range((count - 1) // 2, 0, -1):
        out += [lax.rem(me + j, count), lax.rem(me + count - j, count)]
    return out


def each(count, me, act):
    for other in others(count, me):
        act(other)


def rows(index, size):
    return pl.ds(pl.multiple_of(index * size, size), size)


def kernel(
    nh, nx, nz, groups,
    rate_hbm, skip_hbm, x_hbm, dy_hbm, write_hbm, read_hbm, step_hbm,
    dx_ref, dwrite_ref, dread_ref, dstep_ref,
    rate_ref, skip_ref, write_ref, read_ref, step_ref,
    xg, dyg, bg, cg, pack_out, pack_in,
    cum_ref, wide_cum, grow, wide_step, wide_weight,
    decay_top, decay_low, score_top, score_low, grad_top, grad_low, row_sums,
    summed, dx_buf,
    locals_ref, scan_in, total_send, total_in, prefix, products, turned, ends,
    decay_out, decay_in, line_out, line_in,
    db_half, db_got, db_sum, db_in, dc_half, dc_got, dc_sum, dc_in,
    sems, pack_sems, own_sems,
):
    tok = step_ref.shape[0]
    heads = step_ref.shape[1]
    hl = heads // nh
    nc = nh // 2
    width = hl * WIDTH
    total = nh * tok
    low = total // 2
    pairs = hl // 2
    hh = hl // 2
    part = hh * WIDTH
    tail_rows = tok + hl
    me = lax.axis_index("head")
    at = lax.axis_index("ctx")
    my = me // 2
    core = lax.rem(me, 2)
    sibling = 1 - core
    mx = at // nz
    mz = lax.rem(at, nz)
    of_group = heads // groups

    def by_head(other):
        return {"head": other}

    def by_chip(other):
        return {"head": other * 2 + core}

    def by_core(other):
        return {"head": my * 2 + other}

    def by_z(other):
        return {"ctx": mx * nz + other}

    def by_x(other):
        return {"ctx": other * nz + mz}

    barrier = pltpu.get_barrier_semaphore()

    fetches = [
        pltpu.make_async_copy(src, dst, own_sems.at[3 + i])
        for i, (src, dst) in enumerate(
            (
                (step_hbm, step_ref),
                (write_hbm, write_ref),
                (read_hbm, read_ref),
                (rate_hbm, rate_ref),
                (skip_hbm, skip_ref),
            )
        )
    ]

    def greet(device):
        return lambda other: pl.semaphore_signal(
            barrier, inc=1, device_id=device(other), device_id_type=MESH
        )

    along_y = [(by_head, other) for other in others(nh, me)]
    along_z = [(by_z, other) for other in others(nz, mz)]
    while along_y or along_z:
        for device, other in along_y[:2] + along_z[:1]:
            greet(device)(other)
        along_y, along_z = along_y[2:], along_z[1:]
    if nx > 1:
        each(nx, mx, greet(by_x))
    for fetch in fetches:
        fetch.start()

    def columns(ref):
        return lambda other: ref.at[:, rows(other, width)]

    def some_columns(ref, first, size):
        return lambda other: ref.at[
            :, pl.ds(pl.multiple_of(other * width + first, size), size)
        ]

    def some_block(ref, first, size):
        return lambda other: ref.at[rows(other, tok), first : first + size]

    def block(ref, size):
        return lambda other: ref.at[rows(other, size), :]

    def along_head(src, dst, which, bulk):
        return Exchange(nh, me, by_head, src, dst, sems.at[which], bulk)

    def along_chip(src, dst, which, bulk):
        return Exchange(nc, my, by_chip, src, dst, sems.at[which], bulk)

    def across_core(src, dst, which, bulk):
        return Exchange(2, core, by_core, src, dst, sems.at[which], bulk)

    def first_rows(ref, size, cut=(0, None)):
        if cut[1] is None:
            return lambda n: ref.at[: n * size, :]
        return lambda n: ref.at[: n * size, cut[0] : cut[0] + cut[1]]

    halves = ((0, part), (part, part))
    ex_dy = [
        along_head(
            some_columns(dy_hbm, *cut), some_block(dyg, *cut), i, first_rows(dyg, tok, cut)
        )
        for i, cut in enumerate(halves)
    ]
    ex_dx = [
        along_head(
            some_block(dx_buf, *cut), some_columns(dx_ref, *cut), 2 + i,
            first_rows(dx_buf, tok, cut),
        )
        for i, cut in enumerate(halves)
    ]
    ex_x = [
        along_head(
            some_columns(x_hbm, *cut), some_block(xg, *cut), 4 + i, first_rows(xg, tok, cut)
        )
        for i, cut in enumerate(
            ((0, part), (part, part // 2), (part + part // 2, part // 2))
        )
    ]
    ex_db = along_chip(block(db_sum, tok), block(db_in, tok), 7, first_rows(db_in, tok))
    ex_dc = along_chip(
        block(dc_sum, tail_rows), block(dc_in, tail_rows), 8, first_rows(dc_in, tail_rows)
    )
    pair_pack = across_core(
        lambda t: pack_out.at[my], lambda s: pack_in.at[2 * my + s], 9, lambda n: pack_in.at[0]
    )
    pair_db = across_core(lambda t: db_half.at[t], lambda s: db_got, 10, lambda n: db_got)
    pair_dc = across_core(lambda t: dc_half.at[t], lambda s: dc_got, 11, lambda n: dc_got)
    relay = Exchange(
        nc, my, lambda t: by_core(sibling),
        lambda s: pack_in.at[2 * s + core], lambda s: None, sems.at[12],
        lambda n: pack_in.at[:n],
    )

    def pack_copy(to, slot):
        return pltpu.make_async_remote_copy(
            src_ref=pack_out.at[to],
            dst_ref=pack_in.at[2 * slot + core],
            send_sem=pack_sems.at[0],
            recv_sem=pack_sems.at[1 + slot],
            device_id=by_chip(to),
            device_id_type=MESH,
        )

    def packs_sent():
        if nc > 1:
            pltpu.make_async_remote_copy(
                src_ref=pack_out.at[: nc - 1],
                dst_ref=pack_out.at[: nc - 1],
                send_sem=pack_sems.at[0],
                recv_sem=pack_sems.at[1],
                device_id=by_chip(my),
                device_id_type=MESH,
            ).wait_send()

    grads_a = Unit(0, 1, 0, 0, part, hh)
    grads_b = Unit(1, 1, 1, part, part, hh)
    states_a = Unit(2, 0, 0, 0, part, hh)
    states_b = Unit(3, 0, 1, part, part // 2, hh)
    states_c = Unit(4, 0, 1, part + part // 2, part // 2, hh)
    my_half = lax.rem(mz, 2)

    def rows_of(u, i):
        return pl.ds(pl.multiple_of(u.first + i * u.share, u.share), u.share)

    def my_rows(u):
        return rows_of(u, mz // 2)

    def to_scanner(u):
        return Exchange(
            nz, mz, by_z,
            lambda t: locals_ref.at[u.scan, rows_of(u, t // 2), :],
            lambda s: scan_in.at[u.index, s, : u.share, :],
            sems.at[13 + u.index],
            lambda n: scan_in.at[u.index, :n, : u.share, :],
        )

    def from_scanner(u):
        return Exchange(
            nz, mz, by_z,
            lambda t: turned.at[u.index, t, : u.share, :],
            lambda s: ends.at[u.scan, my_rows(u), :],
            sems.at[18 + u.index],
            lambda n: turned.at[u.index, :n, : u.share, :],
        )

    def ex_total(u):
        return Exchange(
            nx, mx, by_x,
            lambda t: total_send.at[u.index, : u.share, :],
            lambda s: total_in.at[u.index, s, : u.share, :],
            sems.at[23 + u.index],
            lambda n: total_in.at[u.index, :n, : u.share, :],
        )

    ex_decay = Exchange(
        nz, mz, by_z, lambda t: decay_out, lambda s: decay_in.at[s], sems.at[28],
        lambda n: decay_in.at[:n],
    )
    ex_line_decay = Exchange(
        nx, mx, by_x, lambda t: line_out, lambda s: line_in.at[s], sems.at[29],
        lambda n: line_in.at[:n],
    )

    def by_half(half, act):
        @pl.when(my_half == half)
        def _():
            if hh > 1:
                act(hh - 1)

        @pl.when(my_half != half)
        def _():
            act(hh)

    def scanners(half, act):
        for j in range(hh):
            i = lax.rem(mz // 2 + hh // 2 + j, hh)

            @pl.when(2 * i + half != mz)
            def _(z=2 * i + half):
                act(z)

    own_dy = pltpu.make_async_copy(columns(dy_hbm)(me), block(dyg, tok)(me), own_sems.at[0])
    own_x = pltpu.make_async_copy(columns(x_hbm)(me), block(xg, tok)(me), own_sems.at[1])
    own_dy.start()
    own_x.start()
    for fetch in fetches:
        fetch.wait()
    padded = jnp.concatenate([step_ref[...], jnp.zeros((heads - tok, heads), F32)], axis=0)
    flipped = jnp.transpose(padded)
    for target in range(nc):
        g = target * 2 * hl // of_group
        pack_out[target, :tok, :] = write_ref[:, g * STATE : (g + 1) * STATE]
        pack_out[target, tok : 2 * tok, :] = read_ref[:, g * STATE : (g + 1) * STATE]
        first = target * 2 * hl
        pack_out[target, 2 * tok :, :heads] = flipped[first : first + hl, :] + pltpu.roll(
            flipped[first + hl : first + 2 * hl, :], tok, 1
        )
    pack_in[me] = pack_out[my]

    pl.semaphore_wait(barrier, (nh - 1) + (nz - 1) + (nx - 1))

    pair_pack.start(sibling)
    each(nc, my, lambda to: pack_copy(to, my).start())
    for exchange in ex_dy:
        exchange.start_all()

    def hand_on(chip):
        pack_copy(chip, chip).wait_recv()
        pltpu.make_async_remote_copy(
            src_ref=pack_in.at[2 * chip + core],
            dst_ref=pack_in.at[2 * chip + core],
            send_sem=sems.at[12, 0],
            recv_sem=sems.at[12, 1],
            device_id=by_core(sibling),
            device_id_type=MESH,
        ).start()

    each(nc, my, hand_on)
    for exchange in ex_x:
        exchange.start_all()
    pair_pack.arrived()
    relay.arrived()
    bg[...] = pack_in[:, :tok, :].reshape(total, STATE)
    cg[...] = pack_in[:, tok : 2 * tok, :].reshape(total, STATE)

    per_tile = heads // tok
    lane_h = lax.broadcasted_iota(jnp.int32, (hl, heads), 1) // tok
    tiles = []
    for first_source in range(0, nh, per_tile):
        tile = jnp.zeros((hl, heads), F32)
        for source in range(first_source, min(nh, first_source + per_tile)):
            spot = source - first_source
            piece = pack_in[source, 2 * tok :, :heads]
            both = []
            for c in range(2):
                shift = (heads + tok * (spot - c)) % heads
                both.append(pltpu.roll(piece, shift, 1) if shift else piece)
            tile = jnp.where(lane_h == spot, jnp.where(core == 0, both[0], both[1]), tile)
        tiles.append(tile)
    step = jnp.concatenate(tiles, axis=1)[:, :total]
    place = lax.broadcasted_iota(jnp.int32, (hl, 1), 0)
    rate = jnp.zeros((hl, 1), F32)
    for h in range(hl):
        rate = jnp.where(place == h, rate_ref[h], rate)
    lane = lax.broadcasted_iota(jnp.int32, (1, width), 1)
    skip = jnp.zeros((1, width), F32)
    for h in range(hl):
        skip = jnp.where(lane // WIDTH == h, skip_ref[h], skip)
    row_at = lax.broadcasted_iota(jnp.int32, (total, total), 0)
    col_at = lax.broadcasted_iota(jnp.int32, (total, total), 1)
    cumul = exact_nn(-step * rate, (col_at >= row_at).astype(F32))
    cum_ref[...] = cumul
    tail = jnp.exp(cumul[:, total - 1 : total])
    spread = (
        lax.broadcasted_iota(jnp.int32, (hl, width), 1) // WIDTH
        == lax.broadcasted_iota(jnp.int32, (hl, width), 0)
    ).astype(F32)
    wide = exact_tn(cumul, spread)
    wide_cum[...] = wide
    grow[...] = jnp.exp(wide)
    wide_weight[...] = jnp.exp(wide[total - 1 : total, :] - wide)
    wide_step[...] = exact_tn(step, spread)
    decay_out[...] = jnp.broadcast_to(tail, (hl, STATE))
    ex_decay.start_all()
    decay_in[mz] = decay_out[...]
    left_lanes = lax.broadcasted_iota(jnp.int32, (total, 2 * WIDTH), 1) < WIDTH
    later = lax.broadcasted_iota(jnp.int32, (low, low), 1) >= lax.broadcasted_iota(
        jnp.int32, (low, low), 0
    )

    def pair_cols(pair):
        return rows(pair, 2 * WIDTH)

    def masked(gap):
        return jnp.where(later, jnp.exp(jnp.where(later, gap, 0.0)), 0.0)

    def fill_decays(pair, carry):
        here = wide_cum[:, pair_cols(pair)]
        turned_round = pltpu.roll(here, WIDTH, 1)
        for side in range(2):
            h = 2 * pair + side
            col = jnp.where(left_lanes == (side == 0), here, turned_round)[:, :low]
            row = cum_ref[pl.ds(h, 1), :]
            decay_top[h, :, :low] = masked(row[:, :low] - col[:low, :])
            decay_top[h, :, low:] = jnp.exp(row[:, low:] - col[:low, :])
            decay_low[h] = masked(row[:, low:] - col[low:, :])
        return carry

    def send_local(u, local):
        locals_ref[u.scan, u.cut(), :] = local
        scanners(u.half, to_scanner(u).start)

        @pl.when(my_half == u.half)
        def _():
            scan_in[u.index, mz, : u.share, :] = locals_ref[u.scan, my_rows(u), :]

    def line_decays():
        ex_decay.arrived()
        product = decay_in[0]
        for z in range(1, nz):
            product = product * decay_in[z]
        line_out[...] = product
        line_in[mx] = product
        if nx > 1:
            ex_line_decay.start_all()
            ex_line_decay.arrived()

    def scan_line(u):
        @pl.when(my_half == u.half)
        def _():
            head = pl.ds((u.first + mz // 2 * u.share) // WIDTH, 1)
            to_scanner(u).arrived()
            state = jnp.zeros((u.share, STATE), F32)
            product = jnp.ones((1, STATE), F32)
            for lap in range(nz):
                z = nz - 1 - lap if u.scan else lap
                prefix[u.index, z, : u.share, :] = state
                products[u.index, z] = jnp.broadcast_to(product, (8, STATE))
                factor = decay_in[z, head, :]
                state = factor * state + scan_in[u.index, z, : u.share, :]
                product = product * factor
            total_send[u.index, : u.share, :] = state
            if nx > 1:
                ex_total(u).start_all()

    def scan_turn(u):
        @pl.when(my_half == u.half)
        def _():
            head = pl.ds((u.first + mz // 2 * u.share) // WIDTH, 1)
            state = jnp.zeros((u.share, STATE), F32)
            if nx > 1:
                total_in[u.index, mx, : u.share, :] = total_send[u.index, : u.share, :]
                ex_total(u).arrived()
                for lap in range(nx):
                    x = nx - 1 - lap if u.scan else lap
                    before = x > mx if u.scan else x < mx
                    moved = line_in[x, head, :] * state + total_in[u.index, x, : u.share, :]
                    state = jnp.where(before, moved, state)

            def turn(z):
                turned[u.index, z, : u.share, :] = (
                    prefix[u.index, z, : u.share, :] + products[u.index, z, :1, :] * state
                )

            def turn_to(z):
                turn(z)
                from_scanner(u).start(z)

            each(nz, mz, turn_to)
            turn(mz)
            ends[u.scan, my_rows(u), :] = turned[u.index, mz, : u.share, :]

    def scan_arrived(u):
        by_half(u.half, from_scanner(u).arrived)

    def scan_sent(u):
        by_half(u.half, to_scanner(u).sent)

        @pl.when(my_half == u.half)
        def _():
            ex_total(u).sent()
            from_scanner(u).sent()

    def send_grad(u):
        cols = u.cut()
        ex_dy[u.half].arrived()
        send_local(u, tn(grow[:, cols] * dyg[:, cols], cg[...]))

    def send_state(u):
        cols = u.cut()
        ex_x[u.index - 2].arrived()
        send_local(u, tn(wide_weight[:, cols] * wide_step[:, cols] * xg[:, cols], bg[...]))

    def send_dx(u):
        scan_arrived(u)
        cols = u.cut()
        whole = summed[:, cols] + wide_weight[:, cols] * nt(bg[...], ends[1, cols, :])
        summed[:, cols] = whole
        dx_buf[:, cols] = wide_step[:, cols] * whole + skip[:, cols] * dyg[:, cols]
        ex_dx[u.half].start_all()

    own_dy.wait()
    send_grad(grads_a)
    score_top[...] = nt(bg[:low, :], cg[...])
    score_low[...] = nt(bg[low:, :], cg[low:, :])
    lax.fori_loop(0, pairs, fill_decays, 0)

    def fill_summed(pair, carry):
        cols = pair_cols(pair)
        grads = dyg[:, cols]
        heads_of = (2 * pair, 2 * pair + 1)
        above = nn(
            jnp.concatenate([score_top[...] * decay_top[h] for h in heads_of], axis=0), grads
        )
        below = nn(
            jnp.concatenate([score_low[...] * decay_low[h] for h in heads_of], axis=0),
            grads[low:, :],
        )
        summed[:low, cols] = jnp.where(left_lanes[:low, :], above[:low, :], above[low:, :])
        summed[low:, cols] = jnp.where(left_lanes[:low, :], below[:low, :], below[low:, :])
        return carry

    def fill_grad_score(pair, carry):
        cols = pair_cols(pair)
        grads = dyg[:, cols]
        scaled = wide_step[:, cols] * xg[:, cols]
        sides = [jnp.where(left_lanes == (side == 0), scaled, 0.0) for side in range(2)]
        above = nt(jnp.concatenate([one[:low, :] for one in sides], axis=0), grads)
        below = nt(jnp.concatenate([one[low:, :] for one in sides], axis=0), grads[low:, :])
        mixed_top, mixed_low = [], []
        for side in range(2):
            h = 2 * pair + side
            mixed_top.append(above[side * low : (side + 1) * low, :] * decay_top[h])
            mixed_low.append(below[side * low : (side + 1) * low, :] * decay_low[h])
            sums = jnp.sum(mixed_top[side] * score_top[...], axis=0, keepdims=True)
            more = jnp.sum(mixed_low[side] * score_low[...], axis=0, keepdims=True)
            mine = lax.broadcasted_iota(jnp.int32, (hl, low), 0) == h
            row_sums[:, :low] += jnp.where(mine, sums[:, :low], 0.0)
            row_sums[:, low:] += jnp.where(mine, sums[:, low:] + more, 0.0)
        grad_top[...] += mixed_top[0] + mixed_top[1]
        grad_low[...] += mixed_low[0] + mixed_low[1]
        return carry

    grad_top[...] = jnp.zeros_like(grad_top)
    grad_low[...] = jnp.zeros_like(grad_low)
    row_sums[...] = jnp.zeros_like(row_sums)
    line_decays()
    send_grad(grads_b)
    lax.fori_loop(0, pairs // 2, fill_summed, 0)
    scan_line(grads_a)
    own_x.wait()
    send_state(states_a)
    scan_turn(grads_a)
    scan_line(grads_b)
    send_state(states_b)
    send_state(states_c)
    lax.fori_loop(pairs // 2, pairs, fill_summed, 0)
    scan_turn(grads_b)
    scan_line(states_a)
    scan_line(states_b)
    scan_line(states_c)
    scan_turn(states_a)
    send_dx(grads_a)
    lax.fori_loop(0, pairs // 2, fill_grad_score, 0)
    scan_turn(states_b)
    scan_turn(states_c)
    send_dx(grads_b)
    lax.fori_loop(pairs // 2, pairs, fill_grad_score, 0)
    end = ends[1]

    def by_target_core(half, stride, first, value):
        size = value.shape[0] // nh
        for target in range(nh):
            base = (target // 2) * stride + first
            half[target % 2, base : base + size, :] = value[target * size : (target + 1) * size, :]

    from_states = nn(wide_weight[...] * wide_step[...] * xg[...], end)
    by_target_core(db_half, tok, 0, from_states + jnp.concatenate(
        [nn(grad_top[...], cg[...]), nn(grad_low[...], cg[low:, :])], axis=0
    ))
    pair_db.start(sibling)
    along = sum_nt(spread, xg[...] * summed[...])
    from_score = jnp.concatenate(
        [
            tn(grad_top[:, :low], bg[:low, :]),
            tn(grad_top[:, low:], bg[:low, :]) + tn(grad_low[...], bg[low:, :]),
        ],
        axis=0,
    )
    outer = grow[...] * dyg[...]
    made = jnp.sum((end * locals_ref[0]).reshape(hl, WIDTH, STATE), axis=1)
    read_part = from_score
    along_read = row_sums[...] - step * along
    kept = []
    for u in (states_a, states_b, states_c):
        if u is states_b:
            pair_db.arrived()
            db_sum[...] = db_half[core] + db_got[...]
            ex_db.start_all()
            db_in[rows(my, tok), :] = db_sum[rows(my, tok), :]
        scan_arrived(u)
        start = ends[0, u.cut(), :]
        kept.append(
            jnp.sum((end[u.cut(), :] * start).reshape(u.count // WIDTH, WIDTH, STATE), axis=1)
        )
        read_part = read_part + nn(outer[:, u.cut()], start)
        along_read = along_read + sum_nt(
            spread[:, u.cut()], outer[:, u.cut()] * nt(cg[...], start)
        )
    by_target_core(dc_half, tail_rows, 0, read_part)
    kept = jnp.concatenate(kept, axis=0)
    last = jnp.sum(tail * kept + made, axis=1, keepdims=True)
    lane_t = lax.broadcasted_iota(jnp.int32, (hl, total), 1)
    grad_cum = along_read + jnp.where(lane_t == total - 1, last, 0.0)
    grad_log = exact_nn(grad_cum, (row_at >= col_at).astype(F32))
    grad_step = along - rate * grad_log
    for begin in range(0, total, heads):
        piece = grad_step[:, begin : min(total, begin + heads)]
        if piece.shape[1] < heads:
            piece = jnp.concatenate(
                [piece, jnp.zeros((hl, heads - piece.shape[1]), F32)], axis=1
            )
        turns = [pltpu.roll(piece, tok * t, 1) if t else piece for t in range(per_tile)]
        for spot in range(min(per_tile, nh)):
            target = begin // tok + spot
            placed = [turns[(c - spot) % per_tile] for c in range(2)]
            base = (target // 2) * tail_rows + tok
            dc_half[target % 2, base : base + hl, :heads] = jnp.where(
                lane_h == core, jnp.where(core == 0, placed[0], placed[1]), 0.0
            )
    pair_dc.start(sibling)
    pair_dc.arrived()
    dc_sum[...] = dc_half[core] + dc_got[...]
    ex_dc.start_all()
    dc_in[rows(my, tail_rows), :] = dc_sum[rows(my, tail_rows), :]

    share = nc // groups

    def fold(received, stride, out):
        for g in range(groups):
            part = received[g * share * stride : g * share * stride + tok, :]
            for s in range(g * share + 1, (g + 1) * share):
                part = part + received[s * stride : s * stride + tok, :]
            out[:, g * STATE : (g + 1) * STATE] = part

    own_dx = pltpu.make_async_copy(block(dx_buf, tok)(me), columns(dx_ref)(me), own_sems.at[2])
    own_dx.start()
    for exchange in (*ex_dy, *ex_x, *ex_dx, relay, ex_decay, ex_line_decay):
        exchange.sent()
    packs_sent()
    for u in (grads_a, grads_b, states_a, states_b, states_c):
        scan_sent(u)
    for exchange in (pair_pack, pair_db, pair_dc):
        exchange.sent()
    for exchange in ex_dx:
        exchange.arrived()
    ex_db.arrived()
    fold(db_in, tok, dwrite_ref)
    ex_db.sent()
    ex_dc.arrived()
    fold(dc_in, tail_rows, dread_ref)
    by_heads = []
    for chip in range(nc):
        piece = dc_in[chip * tail_rows + tok : (chip + 1) * tail_rows, :heads]
        by_heads += [piece, pltpu.roll(piece, heads - tok, 1)]
    dstep_ref[...] = jnp.transpose(jnp.concatenate(by_heads, axis=0))[:tok, :]
    ex_dc.sent()
    own_dx.wait()


def hand_out(parts, *refs):
    count = len(parts)
    sems = refs[-1]
    copies = []
    for i in range(count):
        wide = refs[i].shape[1] // parts[i]
        for p in range(parts[i]):
            cols = slice(p * wide, (p + 1) * wide)
            copies.append(
                pltpu.make_async_copy(
                    refs[i].at[:, cols], refs[count + i].at[:, cols], sems.at[len(copies)]
                )
            )
    for copy in copies:
        copy.start()
    for copy in copies:
        copy.wait()


def on_device(groups, features, write_proj, read_proj, step_size, decay_rate, skip_weight, upstream):
    nh = lax.axis_size("head")
    tok, heads = step_size.shape
    hl = heads // nh
    nz = hl
    nx = lax.axis_size("ctx") // nz
    width = hl * WIDTH
    nc = nh // 2
    total = nh * tok
    low = total // 2
    vmem = pl.BlockSpec(memory_space=pltpu.VMEM)
    hbm = pl.BlockSpec(memory_space=pltpu.HBM)

    def buf(*shape):
        return pltpu.VMEM(shape, F32)

    results = pl.pallas_call(
        functools.partial(kernel, nh, nx, nz, groups),
        out_shape=(
            jax.ShapeDtypeStruct(features.shape, F32),
            jax.ShapeDtypeStruct(write_proj.shape, F32),
            jax.ShapeDtypeStruct(read_proj.shape, F32),
            jax.ShapeDtypeStruct(step_size.shape, F32),
        ),
        in_specs=[hbm] * 7,
        out_specs=(vmem, vmem, vmem, vmem),
        scratch_shapes=[
            pltpu.SMEM(decay_rate.shape, F32),
            pltpu.SMEM(skip_weight.shape, F32),
            buf(*write_proj.shape),
            buf(*read_proj.shape),
            buf(*step_size.shape),
            buf(total, width),
            buf(total, width),
            buf(total, STATE),
            buf(total, STATE),
            buf(nc, 2 * tok + hl, STATE),
            buf(nh, 2 * tok + hl, STATE),
            buf(hl, total),
            buf(total, width),
            buf(total, width),
            buf(total, width),
            buf(total, width),
            buf(hl, low, total),
            buf(hl, low, low),
            buf(low, total),
            buf(low, low),
            buf(low, total),
            buf(low, low),
            buf(hl, total),
            buf(total, width),
            buf(total, width),
            buf(2, hl * WIDTH, STATE),
            buf(5, nz, WIDTH, STATE),
            buf(5, WIDTH, STATE),
            buf(5, nx, WIDTH, STATE),
            buf(5, nz, WIDTH, STATE),
            buf(5, nz, 8, STATE),
            buf(5, nz, WIDTH, STATE),
            buf(2, hl * WIDTH, STATE),
            buf(hl, STATE),
            buf(nz, hl, STATE),
            buf(hl, STATE),
            buf(nx, hl, STATE),
            buf(2, nc * tok, STATE),
            buf(nc * tok, STATE),
            buf(nc * tok, STATE),
            buf(nc * tok, STATE),
            buf(2, nc * (tok + hl), STATE),
            buf(nc * (tok + hl), STATE),
            buf(nc * (tok + hl), STATE),
            buf(nc * (tok + hl), STATE),
            pltpu.SemaphoreType.DMA((30, 2)),
            pltpu.SemaphoreType.DMA((1 + nc,)),
            pltpu.SemaphoreType.DMA((8,)),
        ],
        compiler_params=pltpu.CompilerParams(
            collective_id=0, has_side_effects=True, vmem_limit_bytes=40 * 1024 * 1024
        ),
        cost_estimate=pl.CostEstimate(
            flops=1_200_000_000, bytes_accessed=8_000_000, transcendentals=600_000
        ),
    )(
        *(
            pltpu.with_memory_space_constraint(a, pltpu.HBM)
            for a in (
                decay_rate, skip_weight, features, upstream, write_proj, read_proj, step_size
            )
        )
    )
    parts = (4, 1, 1, 1)
    return pl.pallas_call(
        functools.partial(hand_out, parts),
        out_shape=tuple(jax.ShapeDtypeStruct(r.shape, F32) for r in results),
        in_specs=[vmem] * len(results),
        out_specs=(hbm,) * len(results),
        scratch_shapes=[pltpu.SemaphoreType.DMA((sum(parts),))],
        compiler_params=pltpu.CompilerParams(vmem_limit_bytes=16 * 1024 * 1024),
        cost_estimate=pl.CostEstimate(flops=0, bytes_accessed=1_200_000, transcendentals=0),
    )(*(pltpu.with_memory_space_constraint(r, pltpu.VMEM) for r in results))


def solution(mesh):
    tokens = P(("ctx", "head"), None)
    return jax.shard_map(
        functools.partial(on_device, GROUPS),
        mesh=mesh,
        in_specs=(tokens, tokens, tokens, tokens, P("head"), P("head"), tokens),
        out_specs=(tokens, tokens, tokens, tokens),
        check_vma=False,
    )
```

```python
import functools

import jax
import jax.numpy as jnp
from jax import lax
from jax.experimental import pallas as pl
from jax.experimental.pallas import tpu as pltpu
from jax.sharding import PartitionSpec as P

STATE = 128
GROUPS = 4
WIDTH = 64
MESH = pl.DeviceIdType.MESH
F32 = jnp.float32
HIGH = lax.Precision.HIGH


def mm(a, b, dims, precision=HIGH):
    return lax.dot_general(
        a, b, (dims, ((), ())), precision=precision, preferred_element_type=F32
    )


def nn(a, b, precision=HIGH):
    return mm(a, b, ((1,), (0,)), precision)


def nt(a, b, precision=HIGH):
    return mm(a, b, ((1,), (1,)), precision)


def tn(a, b, precision=HIGH):
    return mm(a, b, ((0,), (0,)), precision)


def parts_of(a, count):
    out = []
    for _ in range(count):
        piece = a.astype(jnp.bfloat16)
        out.append(piece)
        a = a - piece.astype(F32)
    return out


def exact_nn(a, ones):
    n = a.shape[0]
    stacked = jnp.concatenate([p.astype(F32) for p in parts_of(a, 3)], axis=0)
    out = nn(stacked.astype(jnp.bfloat16), ones.astype(jnp.bfloat16), None)
    return (out[2 * n :] + out[n : 2 * n]) + out[:n]


def exact_tn(a, ones):
    stacked = jnp.concatenate([p.astype(F32) for p in parts_of(a, 3)][::-1], axis=0)
    tall = jnp.concatenate([ones] * 3, axis=0)
    return tn(stacked.astype(jnp.bfloat16), tall.astype(jnp.bfloat16), None)


def sum_nt(ones, b):
    ones = ones.astype(jnp.bfloat16)
    first, second = parts_of(b, 2)
    return nt(ones, second, None) + nt(ones, first, None)


class Unit:
    def __init__(self, index, scan, half, first, count, scanners):
        self.index, self.scan, self.half = index, scan, half
        self.first, self.count, self.share = first, count, count // scanners

    def cut(self):
        return slice(self.first, self.first + self.count)


class Exchange:
    def __init__(self, count, me, device, src, dst, sems, bulk):
        self.count, self.me, self.device = count, me, device
        self.src, self.dst, self.sems, self.bulk = src, dst, sems, bulk

    def start(self, to):
        pltpu.make_async_remote_copy(
            src_ref=self.src(to),
            dst_ref=self.dst(self.me),
            send_sem=self.sems.at[0],
            recv_sem=self.sems.at[1],
            device_id=self.device(to),
            device_id_type=MESH,
        ).start()

    def start_all(self):
        each(self.count, self.me, self.start)

    def whole(self, blocks):
        return pltpu.make_async_remote_copy(
            src_ref=self.bulk(blocks),
            dst_ref=self.bulk(blocks),
            send_sem=self.sems.at[0],
            recv_sem=self.sems.at[1],
            device_id=self.device(lax.rem(self.me + 1, self.count)),
            device_id_type=MESH,
        )

    def arrived(self, blocks=None):
        if self.count > 1:
            self.whole(blocks or self.count - 1).wait_recv()

    def sent(self, blocks=None):
        if self.count > 1:
            self.whole(blocks or self.count - 1).wait_send()


def others(count, me):
    out = [lax.rem(me + count // 2, count)] if count % 2 == 0 else []
    for j in range((count - 1) // 2, 0, -1):
        out += [lax.rem(me + j, count), lax.rem(me + count - j, count)]
    return out


def each(count, me, act):
    for other in others(count, me):
        act(other)


def rows(index, size):
    return pl.ds(pl.multiple_of(index * size, size), size)


def kernel(
    nh, nx, nz, groups,
    rate_hbm, skip_hbm, x_hbm, dy_hbm, write_hbm, read_hbm, step_hbm,
    dx_ref, dwrite_ref, dread_ref, dstep_ref,
    rate_ref, skip_ref, write_ref, read_ref, step_ref,
    xg, dyg, bg, cg, pack_out, pack_in,
    cum_ref, wide_cum, grow, wide_step, wide_weight,
    decay_top, decay_low, score_top, score_low, grad_top, grad_low, row_sums,
    summed, dx_buf,
    locals_ref, scan_in, total_send, total_in, prefix, products, turned, ends,
    decay_out, decay_in, line_out, line_in,
    db_half, db_got, db_sum, db_in, dc_half, dc_got, dc_sum, dc_in,
    sems, pack_sems, own_sems,
):
    tok = step_ref.shape[0]
    heads = step_ref.shape[1]
    hl = heads // nh
    nc = nh // 2
    width = hl * WIDTH
    total = nh * tok
    low = total // 2
    pairs = hl // 2
    hh = hl // 2
    part = hh * WIDTH
    tail_rows = tok + hl
    me = lax.axis_index("head")
    at = lax.axis_index("ctx")
    my = me // 2
    core = lax.rem(me, 2)
    sibling = 1 - core
    mx = at // nz
    mz = lax.rem(at, nz)
    of_group = heads // groups

    def by_head(other):
        return {"head": other}

    def by_chip(other):
        return {"head": other * 2 + core}

    def by_core(other):
        return {"head": my * 2 + other}

    def by_z(other):
        return {"ctx": mx * nz + other}

    def by_x(other):
        return {"ctx": other * nz + mz}

    barrier = pltpu.get_barrier_semaphore()

    fetches = [
        pltpu.make_async_copy(src, dst, own_sems.at[3 + i])
        for i, (src, dst) in enumerate(
            (
                (step_hbm, step_ref),
                (write_hbm, write_ref),
                (read_hbm, read_ref),
                (rate_hbm, rate_ref),
                (skip_hbm, skip_ref),
            )
        )
    ]

    def greet(device):
        return lambda other: pl.semaphore_signal(
            barrier, inc=1, device_id=device(other), device_id_type=MESH
        )

    along_y = [(by_head, other) for other in others(nh, me)]
    along_z = [(by_z, other) for other in others(nz, mz)]
    while along_y or along_z:
        for device, other in along_y[:2] + along_z[:1]:
            greet(device)(other)
        along_y, along_z = along_y[2:], along_z[1:]
    if nx > 1:
        each(nx, mx, greet(by_x))
    for fetch in fetches:
        fetch.start()

    def columns(ref):
        return lambda other: ref.at[:, rows(other, width)]

    def some_columns(ref, first, size):
        return lambda other: ref.at[
            :, pl.ds(pl.multiple_of(other * width + first, size), size)
        ]

    def some_block(ref, first, size):
        return lambda other: ref.at[rows(other, tok), first : first + size]

    def block(ref, size):
        return lambda other: ref.at[rows(other, size), :]

    def along_head(src, dst, which, bulk):
        return Exchange(nh, me, by_head, src, dst, sems.at[which], bulk)

    def along_chip(src, dst, which, bulk):
        return Exchange(nc, my, by_chip, src, dst, sems.at[which], bulk)

    def across_core(src, dst, which, bulk):
        return Exchange(2, core, by_core, src, dst, sems.at[which], bulk)

    def first_rows(ref, size, cut=(0, None)):
        if cut[1] is None:
            return lambda n: ref.at[: n * size, :]
        return lambda n: ref.at[: n * size, cut[0] : cut[0] + cut[1]]

    halves = ((0, part), (part, part))
    ex_dy = [
        along_head(
            some_columns(dy_hbm, *cut), some_block(dyg, *cut), i, first_rows(dyg, tok, cut)
        )
        for i, cut in enumerate(halves)
    ]
    ex_dx = [
        along_head(
            some_block(dx_buf, *cut), some_columns(dx_ref, *cut), 2 + i,
            first_rows(dx_buf, tok, cut),
        )
        for i, cut in enumerate(halves)
    ]
    ex_x = [
        along_head(
            some_columns(x_hbm, *cut), some_block(xg, *cut), 4 + i, first_rows(xg, tok, cut)
        )
        for i, cut in enumerate(
            ((0, part), (part, part // 2), (part + part // 2, part // 2))
        )
    ]
    ex_db = along_chip(block(db_sum, tok), block(db_in, tok), 7, first_rows(db_in, tok))
    ex_dc = along_chip(
        block(dc_sum, tail_rows), block(dc_in, tail_rows), 8, first_rows(dc_in, tail_rows)
    )
    pair_pack = across_core(
        lambda t: pack_out.at[my], lambda s: pack_in.at[2 * my + s], 9, lambda n: pack_in.at[0]
    )
    pair_db = across_core(lambda t: db_half.at[t], lambda s: db_got, 10, lambda n: db_got)
    pair_dc = across_core(lambda t: dc_half.at[t], lambda s: dc_got, 11, lambda n: dc_got)
    relay = Exchange(
        nc, my, lambda t: by_core(sibling),
        lambda s: pack_in.at[2 * s + core], lambda s: None, sems.at[12],
        lambda n: pack_in.at[:n],
    )

    def pack_copy(to, slot):
        return pltpu.make_async_remote_copy(
            src_ref=pack_out.at[to],
            dst_ref=pack_in.at[2 * slot + core],
            send_sem=pack_sems.at[0],
            recv_sem=pack_sems.at[1 + slot],
            device_id=by_chip(to),
            device_id_type=MESH,
        )

    def packs_sent():
        if nc > 1:
            pltpu.make_async_remote_copy(
                src_ref=pack_out.at[: nc - 1],
                dst_ref=pack_out.at[: nc - 1],
                send_sem=pack_sems.at[0],
                recv_sem=pack_sems.at[1],
                device_id=by_chip(my),
                device_id_type=MESH,
            ).wait_send()

    grads_a = Unit(0, 1, 0, 0, part, hh)
    grads_b = Unit(1, 1, 1, part, part, hh)
    states_a = Unit(2, 0, 0, 0, part, hh)
    states_b = Unit(3, 0, 1, part, part // 2, hh)
    states_c = Unit(4, 0, 1, part + part // 2, part // 2, hh)
    my_half = lax.rem(mz, 2)

    def rows_of(u, i):
        return pl.ds(pl.multiple_of(u.first + i * u.share, u.share), u.share)

    def my_rows(u):
        return rows_of(u, mz // 2)

    def to_scanner(u):
        return Exchange(
            nz, mz, by_z,
            lambda t: locals_ref.at[u.scan, rows_of(u, t // 2), :],
            lambda s: scan_in.at[u.index, s, : u.share, :],
            sems.at[13 + u.index],
            lambda n: scan_in.at[u.index, :n, : u.share, :],
        )

    def from_scanner(u):
        return Exchange(
            nz, mz, by_z,
            lambda t: turned.at[u.index, t, : u.share, :],
            lambda s: ends.at[u.scan, my_rows(u), :],
            sems.at[18 + u.index],
            lambda n: turned.at[u.index, :n, : u.share, :],
        )

    def ex_total(u):
        return Exchange(
            nx, mx, by_x,
            lambda t: total_send.at[u.index, : u.share, :],
            lambda s: total_in.at[u.index, s, : u.share, :],
            sems.at[23 + u.index],
            lambda n: total_in.at[u.index, :n, : u.share, :],
        )

    ex_decay = Exchange(
        nz, mz, by_z, lambda t: decay_out, lambda s: decay_in.at[s], sems.at[28],
        lambda n: decay_in.at[:n],
    )
    ex_line_decay = Exchange(
        nx, mx, by_x, lambda t: line_out, lambda s: line_in.at[s], sems.at[29],
        lambda n: line_in.at[:n],
    )

    def by_half(half, act):
        @pl.when(my_half == half)
        def _():
            if hh > 1:
                act(hh - 1)

        @pl.when(my_half != half)
        def _():
            act(hh)

    def scanners(half, act):
        for j in range(hh):
            i = lax.rem(mz // 2 + hh // 2 + j, hh)

            @pl.when(2 * i + half != mz)
            def _(z=2 * i + half):
                act(z)

    own_dy = pltpu.make_async_copy(columns(dy_hbm)(me), block(dyg, tok)(me), own_sems.at[0])
    own_x = pltpu.make_async_copy(columns(x_hbm)(me), block(xg, tok)(me), own_sems.at[1])
    own_dy.start()
    own_x.start()
    for fetch in fetches:
        fetch.wait()
    padded = jnp.concatenate([step_ref[...], jnp.zeros((heads - tok, heads), F32)], axis=0)
    flipped = jnp.transpose(padded)
    for target in range(nc):
        g = target * 2 * hl // of_group
        pack_out[target, :tok, :] = write_ref[:, g * STATE : (g + 1) * STATE]
        pack_out[target, tok : 2 * tok, :] = read_ref[:, g * STATE : (g + 1) * STATE]
        first = target * 2 * hl
        pack_out[target, 2 * tok :, :heads] = flipped[first : first + hl, :] + pltpu.roll(
            flipped[first + hl : first + 2 * hl, :], tok, 1
        )
    pack_in[me] = pack_out[my]

    pl.semaphore_wait(barrier, (nh - 1) + (nz - 1) + (nx - 1))

    pair_pack.start(sibling)
    each(nc, my, lambda to: pack_copy(to, my).start())
    for exchange in (*ex_dy, ex_x[0]):
        exchange.start_all()

    def hand_on(chip):
        pack_copy(chip, chip).wait_recv()
        pltpu.make_async_remote_copy(
            src_ref=pack_in.at[2 * chip + core],
            dst_ref=pack_in.at[2 * chip + core],
            send_sem=sems.at[12, 0],
            recv_sem=sems.at[12, 1],
            device_id=by_core(sibling),
            device_id_type=MESH,
        ).start()

    each(nc, my, hand_on)
    for exchange in ex_x[1:]:
        exchange.start_all()
    pair_pack.arrived()
    relay.arrived()
    bg[...] = pack_in[:, :tok, :].reshape(total, STATE)
    cg[...] = pack_in[:, tok : 2 * tok, :].reshape(total, STATE)

    per_tile = heads // tok
    lane_h = lax.broadcasted_iota(jnp.int32, (hl, heads), 1) // tok
    tiles = []
    for first_source in range(0, nh, per_tile):
        tile = jnp.zeros((hl, heads), F32)
        for source in range(first_source, min(nh, first_source + per_tile)):
            spot = source - first_source
            piece = pack_in[source, 2 * tok :, :heads]
            both = []
            for c in range(2):
                shift = (heads + tok * (spot - c)) % heads
                both.append(pltpu.roll(piece, shift, 1) if shift else piece)
            tile = jnp.where(lane_h == spot, jnp.where(core == 0, both[0], both[1]), tile)
        tiles.append(tile)
    step = jnp.concatenate(tiles, axis=1)[:, :total]
    place = lax.broadcasted_iota(jnp.int32, (hl, 1), 0)
    rate = jnp.zeros((hl, 1), F32)
    for h in range(hl):
        rate = jnp.where(place == h, rate_ref[h], rate)
    lane = lax.broadcasted_iota(jnp.int32, (1, width), 1)
    skip = jnp.zeros((1, width), F32)
    for h in range(hl):
        skip = jnp.where(lane // WIDTH == h, skip_ref[h], skip)
    row_at = lax.broadcasted_iota(jnp.int32, (total, total), 0)
    col_at = lax.broadcasted_iota(jnp.int32, (total, total), 1)
    cumul = exact_nn(-step * rate, (col_at >= row_at).astype(F32))
    cum_ref[...] = cumul
    tail = jnp.exp(cumul[:, total - 1 : total])
    spread = (
        lax.broadcasted_iota(jnp.int32, (hl, width), 1) // WIDTH
        == lax.broadcasted_iota(jnp.int32, (hl, width), 0)
    ).astype(F32)
    wide = exact_tn(cumul, spread)
    wide_cum[...] = wide
    grow[...] = jnp.exp(wide)
    wide_weight[...] = jnp.exp(wide[total - 1 : total, :] - wide)
    wide_step[...] = exact_tn(step, spread)
    decay_out[...] = jnp.broadcast_to(tail, (hl, STATE))
    ex_decay.start_all()
    decay_in[mz] = decay_out[...]
    left_lanes = lax.broadcasted_iota(jnp.int32, (total, 2 * WIDTH), 1) < WIDTH
    later = lax.broadcasted_iota(jnp.int32, (low, low), 1) >= lax.broadcasted_iota(
        jnp.int32, (low, low), 0
    )

    def pair_cols(pair):
        return rows(pair, 2 * WIDTH)

    def masked(gap):
        return jnp.where(later, jnp.exp(jnp.where(later, gap, 0.0)), 0.0)

    def fill_decays(pair, carry):
        here = wide_cum[:, pair_cols(pair)]
        turned_round = pltpu.roll(here, WIDTH, 1)
        for side in range(2):
            h = 2 * pair + side
            col = jnp.where(left_lanes == (side == 0), here, turned_round)[:, :low]
            row = cum_ref[pl.ds(h, 1), :]
            decay_top[h, :, :low] = masked(row[:, :low] - col[:low, :])
            decay_top[h, :, low:] = jnp.exp(row[:, low:] - col[:low, :])
            decay_low[h] = masked(row[:, low:] - col[low:, :])
        return carry

    def send_local(u, local):
        locals_ref[u.scan, u.cut(), :] = local
        scanners(u.half, to_scanner(u).start)

        @pl.when(my_half == u.half)
        def _():
            scan_in[u.index, mz, : u.share, :] = locals_ref[u.scan, my_rows(u), :]

    def line_decays():
        ex_decay.arrived()
        product = decay_in[0]
        for z in range(1, nz):
            product = product * decay_in[z]
        line_out[...] = product
        line_in[mx] = product
        if nx > 1:
            ex_line_decay.start_all()

    def scan_line(u):
        @pl.when(my_half == u.half)
        def _():
            head = pl.ds((u.first + mz // 2 * u.share) // WIDTH, 1)
            to_scanner(u).arrived()
            state = jnp.zeros((u.share, STATE), F32)
            product = jnp.ones((1, STATE), F32)
            for lap in range(nz):
                z = nz - 1 - lap if u.scan else lap
                prefix[u.index, z, : u.share, :] = state
                products[u.index, z] = jnp.broadcast_to(product, (8, STATE))
                factor = decay_in[z, head, :]
                state = factor * state + scan_in[u.index, z, : u.share, :]
                product = product * factor
            total_send[u.index, : u.share, :] = state
            if nx > 1:
                ex_total(u).start_all()

    def scan_turn(u):
        @pl.when(my_half == u.half)
        def _():
            head = pl.ds((u.first + mz // 2 * u.share) // WIDTH, 1)
            state = jnp.zeros((u.share, STATE), F32)
            if nx > 1:
                total_in[u.index, mx, : u.share, :] = total_send[u.index, : u.share, :]
                ex_total(u).arrived()
                for lap in range(nx):
                    x = nx - 1 - lap if u.scan else lap
                    before = x > mx if u.scan else x < mx
                    moved = line_in[x, head, :] * state + total_in[u.index, x, : u.share, :]
                    state = jnp.where(before, moved, state)

            def turn(z):
                turned[u.index, z, : u.share, :] = (
                    prefix[u.index, z, : u.share, :] + products[u.index, z, :1, :] * state
                )

            def turn_to(z):
                turn(z)
                from_scanner(u).start(z)

            each(nz, mz, turn_to)
            turn(mz)
            ends[u.scan, my_rows(u), :] = turned[u.index, mz, : u.share, :]

    def scan_arrived(u):
        by_half(u.half, from_scanner(u).arrived)

    def scan_sent(u):
        by_half(u.half, to_scanner(u).sent)

        @pl.when(my_half == u.half)
        def _():
            ex_total(u).sent()
            from_scanner(u).sent()

    def send_grad(u):
        cols = u.cut()
        ex_dy[u.half].arrived()
        send_local(u, tn(grow[:, cols] * dyg[:, cols], cg[...]))

    def send_state(u):
        cols = u.cut()
        ex_x[u.index - 2].arrived()
        send_local(u, tn(wide_weight[:, cols] * wide_step[:, cols] * xg[:, cols], bg[...]))

    def send_dx(u):
        scan_arrived(u)
        cols = u.cut()
        whole = summed[:, cols] + wide_weight[:, cols] * nt(bg[...], ends[1, cols, :])
        summed[:, cols] = whole
        dx_buf[:, cols] = wide_step[:, cols] * whole + skip[:, cols] * dyg[:, cols]
        ex_dx[u.half].start_all()

    own_dy.wait()
    send_grad(grads_a)
    score_top[...] = nt(bg[:low, :], cg[...])
    score_low[...] = nt(bg[low:, :], cg[low:, :])
    lax.fori_loop(0, pairs, fill_decays, 0)

    def fill_summed(pair, carry):
        cols = pair_cols(pair)
        grads = dyg[:, cols]
        heads_of = (2 * pair, 2 * pair + 1)
        above = nn(
            jnp.concatenate([score_top[...] * decay_top[h] for h in heads_of], axis=0), grads
        )
        below = nn(
            jnp.concatenate([score_low[...] * decay_low[h] for h in heads_of], axis=0),
            grads[low:, :],
        )
        summed[:low, cols] = jnp.where(left_lanes[:low, :], above[:low, :], above[low:, :])
        summed[low:, cols] = jnp.where(left_lanes[:low, :], below[:low, :], below[low:, :])
        return carry

    def fill_grad_score(pair, carry):
        cols = pair_cols(pair)
        grads = dyg[:, cols]
        scaled = wide_step[:, cols] * xg[:, cols]
        sides = [jnp.where(left_lanes == (side == 0), scaled, 0.0) for side in range(2)]
        above = nt(jnp.concatenate([one[:low, :] for one in sides], axis=0), grads)
        below = nt(jnp.concatenate([one[low:, :] for one in sides], axis=0), grads[low:, :])
        mixed_top, mixed_low = [], []
        for side in range(2):
            h = 2 * pair + side
            mixed_top.append(above[side * low : (side + 1) * low, :] * decay_top[h])
            mixed_low.append(below[side * low : (side + 1) * low, :] * decay_low[h])
            sums = jnp.sum(mixed_top[side] * score_top[...], axis=0, keepdims=True)
            more = jnp.sum(mixed_low[side] * score_low[...], axis=0, keepdims=True)
            mine = lax.broadcasted_iota(jnp.int32, (hl, low), 0) == h
            row_sums[:, :low] += jnp.where(mine, sums[:, :low], 0.0)
            row_sums[:, low:] += jnp.where(mine, sums[:, low:] + more, 0.0)
        grad_top[...] += mixed_top[0] + mixed_top[1]
        grad_low[...] += mixed_low[0] + mixed_low[1]
        return carry

    grad_top[...] = jnp.zeros_like(grad_top)
    grad_low[...] = jnp.zeros_like(grad_low)
    row_sums[...] = jnp.zeros_like(row_sums)
    line_decays()
    send_grad(grads_b)
    lax.fori_loop(0, pairs // 2, fill_summed, 0)
    scan_line(grads_a)
    own_x.wait()
    send_state(states_a)
    send_state(states_b)
    send_state(states_c)
    if nx > 1:
        ex_line_decay.arrived()
    scan_turn(grads_a)
    scan_line(grads_b)
    lax.fori_loop(pairs // 2, pairs, fill_summed, 0)
    scan_turn(grads_b)
    scan_line(states_a)
    scan_line(states_b)
    scan_line(states_c)
    scan_turn(states_a)
    send_dx(grads_a)
    lax.fori_loop(0, pairs // 2, fill_grad_score, 0)
    scan_turn(states_b)
    scan_turn(states_c)
    send_dx(grads_b)
    lax.fori_loop(pairs // 2, pairs, fill_grad_score, 0)
    end = ends[1]

    def by_target_core(half, stride, first, value):
        size = value.shape[0] // nh
        for target in range(nh):
            base = (target // 2) * stride + first
            half[target % 2, base : base + size, :] = value[target * size : (target + 1) * size, :]

    from_states = nn(wide_weight[...] * wide_step[...] * xg[...], end)
    by_target_core(db_half, tok, 0, from_states + jnp.concatenate(
        [nn(grad_top[...], cg[...]), nn(grad_low[...], cg[low:, :])], axis=0
    ))
    pair_db.start(sibling)
    along = sum_nt(spread, xg[...] * summed[...])
    from_score = jnp.concatenate(
        [
            tn(grad_top[:, :low], bg[:low, :]),
            tn(grad_top[:, low:], bg[:low, :]) + tn(grad_low[...], bg[low:, :]),
        ],
        axis=0,
    )
    outer = grow[...] * dyg[...]
    made = jnp.sum((end * locals_ref[0]).reshape(hl, WIDTH, STATE), axis=1)
    read_part = from_score
    along_read = row_sums[...] - step * along
    kept = []
    for u in (states_a, states_b, states_c):
        if u is states_b:
            pair_db.arrived()
            db_sum[...] = db_half[core] + db_got[...]
            ex_db.start_all()
            db_in[rows(my, tok), :] = db_sum[rows(my, tok), :]
        scan_arrived(u)
        start = ends[0, u.cut(), :]
        kept.append(
            jnp.sum((end[u.cut(), :] * start).reshape(u.count // WIDTH, WIDTH, STATE), axis=1)
        )
        read_part = read_part + nn(outer[:, u.cut()], start)
        along_read = along_read + sum_nt(
            spread[:, u.cut()], outer[:, u.cut()] * nt(cg[...], start)
        )
    by_target_core(dc_half, tail_rows, 0, read_part)
    kept = jnp.concatenate(kept, axis=0)
    last = jnp.sum(tail * kept + made, axis=1, keepdims=True)
    lane_t = lax.broadcasted_iota(jnp.int32, (hl, total), 1)
    grad_cum = along_read + jnp.where(lane_t == total - 1, last, 0.0)
    grad_log = exact_nn(grad_cum, (row_at >= col_at).astype(F32))
    grad_step = along - rate * grad_log
    for begin in range(0, total, heads):
        piece = grad_step[:, begin : min(total, begin + heads)]
        if piece.shape[1] < heads:
            piece = jnp.concatenate(
                [piece, jnp.zeros((hl, heads - piece.shape[1]), F32)], axis=1
            )
        turns = [pltpu.roll(piece, tok * t, 1) if t else piece for t in range(per_tile)]
        for spot in range(min(per_tile, nh)):
            target = begin // tok + spot
            placed = [turns[(c - spot) % per_tile] for c in range(2)]
            base = (target // 2) * tail_rows + tok
            dc_half[target % 2, base : base + hl, :heads] = jnp.where(
                lane_h == core, jnp.where(core == 0, placed[0], placed[1]), 0.0
            )
    pair_dc.start(sibling)
    pair_dc.arrived()
    dc_sum[...] = dc_half[core] + dc_got[...]
    ex_dc.start_all()
    dc_in[rows(my, tail_rows), :] = dc_sum[rows(my, tail_rows), :]

    share = nc // groups

    def fold(received, stride, out):
        for g in range(groups):
            part = received[g * share * stride : g * share * stride + tok, :]
            for s in range(g * share + 1, (g + 1) * share):
                part = part + received[s * stride : s * stride + tok, :]
            out[:, g * STATE : (g + 1) * STATE] = part

    own_dx = pltpu.make_async_copy(block(dx_buf, tok)(me), columns(dx_ref)(me), own_sems.at[2])
    own_dx.start()
    for exchange in (*ex_dy, *ex_x, *ex_dx, relay, ex_decay, ex_line_decay):
        exchange.sent()
    packs_sent()
    for u in (grads_a, grads_b, states_a, states_b, states_c):
        scan_sent(u)
    for exchange in (pair_pack, pair_db, pair_dc):
        exchange.sent()
    for exchange in ex_dx:
        exchange.arrived()
    ex_db.arrived()
    fold(db_in, tok, dwrite_ref)
    ex_db.sent()
    ex_dc.arrived()
    fold(dc_in, tail_rows, dread_ref)
    by_heads = []
    for chip in range(nc):
        piece = dc_in[chip * tail_rows + tok : (chip + 1) * tail_rows, :heads]
        by_heads += [piece, pltpu.roll(piece, heads - tok, 1)]
    dstep_ref[...] = jnp.transpose(jnp.concatenate(by_heads, axis=0))[:tok, :]
    ex_dc.sent()
    own_dx.wait()


def hand_out(parts, *refs):
    count = len(parts)
    sems = refs[-1]
    copies = []
    for i in range(count):
        wide = refs[i].shape[1] // parts[i]
        for p in range(parts[i]):
            cols = slice(p * wide, (p + 1) * wide)
            copies.append(
                pltpu.make_async_copy(
                    refs[i].at[:, cols], refs[count + i].at[:, cols], sems.at[len(copies)]
                )
            )
    for copy in copies:
        copy.start()
    for copy in copies:
        copy.wait()


def on_device(groups, features, write_proj, read_proj, step_size, decay_rate, skip_weight, upstream):
    nh = lax.axis_size("head")
    tok, heads = step_size.shape
    hl = heads // nh
    nz = hl
    nx = lax.axis_size("ctx") // nz
    width = hl * WIDTH
    nc = nh // 2
    total = nh * tok
    low = total // 2
    vmem = pl.BlockSpec(memory_space=pltpu.VMEM)
    hbm = pl.BlockSpec(memory_space=pltpu.HBM)

    def buf(*shape):
        return pltpu.VMEM(shape, F32)

    results = pl.pallas_call(
        functools.partial(kernel, nh, nx, nz, groups),
        out_shape=(
            jax.ShapeDtypeStruct(features.shape, F32),
            jax.ShapeDtypeStruct(write_proj.shape, F32),
            jax.ShapeDtypeStruct(read_proj.shape, F32),
            jax.ShapeDtypeStruct(step_size.shape, F32),
        ),
        in_specs=[hbm] * 7,
        out_specs=(vmem, vmem, vmem, vmem),
        scratch_shapes=[
            pltpu.SMEM(decay_rate.shape, F32),
            pltpu.SMEM(skip_weight.shape, F32),
            buf(*write_proj.shape),
            buf(*read_proj.shape),
            buf(*step_size.shape),
            buf(total, width),
            buf(total, width),
            buf(total, STATE),
            buf(total, STATE),
            buf(nc, 2 * tok + hl, STATE),
            buf(nh, 2 * tok + hl, STATE),
            buf(hl, total),
            buf(total, width),
            buf(total, width),
            buf(total, width),
            buf(total, width),
            buf(hl, low, total),
            buf(hl, low, low),
            buf(low, total),
            buf(low, low),
            buf(low, total),
            buf(low, low),
            buf(hl, total),
            buf(total, width),
            buf(total, width),
            buf(2, hl * WIDTH, STATE),
            buf(5, nz, WIDTH, STATE),
            buf(5, WIDTH, STATE),
            buf(5, nx, WIDTH, STATE),
            buf(5, nz, WIDTH, STATE),
            buf(5, nz, 8, STATE),
            buf(5, nz, WIDTH, STATE),
            buf(2, hl * WIDTH, STATE),
            buf(hl, STATE),
            buf(nz, hl, STATE),
            buf(hl, STATE),
            buf(nx, hl, STATE),
            buf(2, nc * tok, STATE),
            buf(nc * tok, STATE),
            buf(nc * tok, STATE),
            buf(nc * tok, STATE),
            buf(2, nc * (tok + hl), STATE),
            buf(nc * (tok + hl), STATE),
            buf(nc * (tok + hl), STATE),
            buf(nc * (tok + hl), STATE),
            pltpu.SemaphoreType.DMA((30, 2)),
            pltpu.SemaphoreType.DMA((1 + nc,)),
            pltpu.SemaphoreType.DMA((8,)),
        ],
        compiler_params=pltpu.CompilerParams(
            collective_id=0, has_side_effects=True, vmem_limit_bytes=40 * 1024 * 1024
        ),
        cost_estimate=pl.CostEstimate(
            flops=1_200_000_000, bytes_accessed=8_000_000, transcendentals=600_000
        ),
    )(
        *(
            pltpu.with_memory_space_constraint(a, pltpu.HBM)
            for a in (
                decay_rate, skip_weight, features, upstream, write_proj, read_proj, step_size
            )
        )
    )
    parts = (4, 1, 1, 1)
    return pl.pallas_call(
        functools.partial(hand_out, parts),
        out_shape=tuple(jax.ShapeDtypeStruct(r.shape, F32) for r in results),
        in_specs=[vmem] * len(results),
        out_specs=(hbm,) * len(results),
        scratch_shapes=[pltpu.SemaphoreType.DMA((sum(parts),))],
        compiler_params=pltpu.CompilerParams(vmem_limit_bytes=16 * 1024 * 1024),
        cost_estimate=pl.CostEstimate(flops=0, bytes_accessed=1_200_000, transcendentals=0),
    )(*(pltpu.with_memory_space_constraint(r, pltpu.VMEM) for r in results))


def solution(mesh):
    tokens = P(("ctx", "head"), None)
    return jax.shard_map(
        functools.partial(on_device, GROUPS),
        mesh=mesh,
        in_specs=(tokens, tokens, tokens, tokens, P("head"), P("head"), tokens),
        out_specs=(tokens, tokens, tokens, tokens),
        check_vma=False,
    )
```

```python
import functools

import jax
import jax.numpy as jnp
from jax import lax
from jax.experimental import pallas as pl
from jax.experimental.pallas import tpu as pltpu
from jax.sharding import PartitionSpec as P

STATE = 128
GROUPS = 4
WIDTH = 64
MESH = pl.DeviceIdType.MESH
F32 = jnp.float32
HIGH = lax.Precision.HIGH


def mm(a, b, dims, precision=HIGH):
    return lax.dot_general(
        a, b, (dims, ((), ())), precision=precision, preferred_element_type=F32
    )


def nn(a, b, precision=HIGH):
    return mm(a, b, ((1,), (0,)), precision)


def nt(a, b, precision=HIGH):
    return mm(a, b, ((1,), (1,)), precision)


def tn(a, b, precision=HIGH):
    return mm(a, b, ((0,), (0,)), precision)


def parts_of(a, count):
    out = []
    for _ in range(count):
        piece = a.astype(jnp.bfloat16)
        out.append(piece)
        a = a - piece.astype(F32)
    return out


def exact_nn(a, ones):
    n = a.shape[0]
    stacked = jnp.concatenate([p.astype(F32) for p in parts_of(a, 3)], axis=0)
    out = nn(stacked.astype(jnp.bfloat16), ones.astype(jnp.bfloat16), None)
    return (out[2 * n :] + out[n : 2 * n]) + out[:n]


def exact_tn(a, ones):
    stacked = jnp.concatenate([p.astype(F32) for p in parts_of(a, 3)][::-1], axis=0)
    tall = jnp.concatenate([ones] * 3, axis=0)
    return tn(stacked.astype(jnp.bfloat16), tall.astype(jnp.bfloat16), None)


def sum_nt(ones, b):
    ones = ones.astype(jnp.bfloat16)
    first, second = parts_of(b, 2)
    return nt(ones, second, None) + nt(ones, first, None)


class Unit:
    def __init__(self, index, scan, half, first, count, scanners):
        self.index, self.scan, self.half = index, scan, half
        self.first, self.count, self.share = first, count, count // scanners

    def cut(self):
        return slice(self.first, self.first + self.count)


class Exchange:
    def __init__(self, count, me, device, src, dst, sems, bulk):
        self.count, self.me, self.device = count, me, device
        self.src, self.dst, self.sems, self.bulk = src, dst, sems, bulk

    def start(self, to):
        pltpu.make_async_remote_copy(
            src_ref=self.src(to),
            dst_ref=self.dst(self.me),
            send_sem=self.sems.at[0],
            recv_sem=self.sems.at[1],
            device_id=self.device(to),
            device_id_type=MESH,
        ).start()

    def start_all(self):
        each(self.count, self.me, self.start)

    def whole(self, blocks):
        return pltpu.make_async_remote_copy(
            src_ref=self.bulk(blocks),
            dst_ref=self.bulk(blocks),
            send_sem=self.sems.at[0],
            recv_sem=self.sems.at[1],
            device_id=self.device(lax.rem(self.me + 1, self.count)),
            device_id_type=MESH,
        )

    def arrived(self, blocks=None):
        if self.count > 1:
            self.whole(blocks or self.count - 1).wait_recv()

    def sent(self, blocks=None):
        if self.count > 1:
            self.whole(blocks or self.count - 1).wait_send()


def others(count, me):
    out = [lax.rem(me + count // 2, count)] if count % 2 == 0 else []
    for j in range((count - 1) // 2, 0, -1):
        out += [lax.rem(me + j, count), lax.rem(me + count - j, count)]
    return out


def each(count, me, act):
    for other in others(count, me):
        act(other)


def rows(index, size):
    return pl.ds(pl.multiple_of(index * size, size), size)


def kernel(
    nh, nx, nz, groups,
    rate_hbm, skip_hbm, x_hbm, dy_hbm, write_hbm, read_hbm, step_hbm,
    dx_ref, dwrite_ref, dread_ref, dstep_ref,
    rate_ref, skip_ref, write_ref, read_ref, step_ref, x_ref, dy_ref,
    xg, dyg, bg, cg, pack_out, pack_in,
    cum_ref, wide_cum, grow, wide_step, wide_weight,
    decay_top, decay_low, score_top, score_low, grad_top, grad_low, row_sums,
    summed, dx_buf,
    locals_ref, scan_in, total_send, total_in, prefix, products, turned, ends,
    decay_out, decay_in, line_out, line_in,
    db_half, db_got, db_sum, db_in, dc_half, dc_got, dc_sum, dc_in,
    sems, pack_sems, own_sems,
):
    tok = step_ref.shape[0]
    heads = step_ref.shape[1]
    hl = heads // nh
    nc = nh // 2
    width = hl * WIDTH
    total = nh * tok
    low = total // 2
    pairs = hl // 2
    hh = hl // 2
    part = hh * WIDTH
    tail_rows = tok + hl
    me = lax.axis_index("head")
    at = lax.axis_index("ctx")
    my = me // 2
    core = lax.rem(me, 2)
    sibling = 1 - core
    mx = at // nz
    mz = lax.rem(at, nz)
    of_group = heads // groups

    def by_head(other):
        return {"head": other}

    def by_chip(other):
        return {"head": other * 2 + core}

    def by_core(other):
        return {"head": my * 2 + other}

    def by_z(other):
        return {"ctx": mx * nz + other}

    def by_x(other):
        return {"ctx": other * nz + mz}

    barrier = pltpu.get_barrier_semaphore()

    fetches = [
        pltpu.make_async_copy(src, dst, own_sems.at[3 + i])
        for i, (src, dst) in enumerate(
            (
                (step_hbm, step_ref),
                (write_hbm, write_ref),
                (read_hbm, read_ref),
                (rate_hbm, rate_ref),
                (skip_hbm, skip_ref),
            )
        )
    ]

    def greet(device):
        return lambda other: pl.semaphore_signal(
            barrier, inc=1, device_id=device(other), device_id_type=MESH
        )

    along_y = [(by_head, other) for other in others(nh, me)]
    along_z = [(by_z, other) for other in others(nz, mz)]
    while along_y or along_z:
        for device, other in along_y[:2] + along_z[:1]:
            greet(device)(other)
        along_y, along_z = along_y[2:], along_z[1:]
    if nx > 1:
        each(nx, mx, greet(by_x))
    fetch_dy = pltpu.make_async_copy(dy_hbm, dy_ref, own_sems.at[8])
    fetch_x = pltpu.make_async_copy(x_hbm, x_ref, own_sems.at[9])
    for fetch in (*fetches, fetch_dy, fetch_x):
        fetch.start()

    def columns(ref):
        return lambda other: ref.at[:, rows(other, width)]

    def some_columns(ref, first, size):
        return lambda other: ref.at[
            :, pl.ds(pl.multiple_of(other * width + first, size), size)
        ]

    def some_block(ref, first, size):
        return lambda other: ref.at[rows(other, tok), first : first + size]

    def block(ref, size):
        return lambda other: ref.at[rows(other, size), :]

    def along_head(src, dst, which, bulk):
        return Exchange(nh, me, by_head, src, dst, sems.at[which], bulk)

    def along_chip(src, dst, which, bulk):
        return Exchange(nc, my, by_chip, src, dst, sems.at[which], bulk)

    def across_core(src, dst, which, bulk):
        return Exchange(2, core, by_core, src, dst, sems.at[which], bulk)

    def first_rows(ref, size, cut=(0, None)):
        if cut[1] is None:
            return lambda n: ref.at[: n * size, :]
        return lambda n: ref.at[: n * size, cut[0] : cut[0] + cut[1]]

    halves = ((0, part), (part, part))
    ex_dy = [
        along_head(
            some_columns(dy_ref, *cut), some_block(dyg, *cut), i, first_rows(dyg, tok, cut)
        )
        for i, cut in enumerate(halves)
    ]
    ex_dx = [
        along_head(
            some_block(dx_buf, *cut), some_columns(dx_ref, *cut), 2 + i,
            first_rows(dx_buf, tok, cut),
        )
        for i, cut in enumerate(halves)
    ]
    ex_x = [
        along_head(
            some_columns(x_ref, *cut), some_block(xg, *cut), 4 + i, first_rows(xg, tok, cut)
        )
        for i, cut in enumerate(
            ((0, part), (part, part // 2), (part + part // 2, part // 2))
        )
    ]
    ex_db = along_chip(block(db_sum, tok), block(db_in, tok), 7, first_rows(db_in, tok))
    ex_dc = along_chip(
        block(dc_sum, tail_rows), block(dc_in, tail_rows), 8, first_rows(dc_in, tail_rows)
    )
    pair_pack = across_core(
        lambda t: pack_out.at[my], lambda s: pack_in.at[2 * my + s], 9, lambda n: pack_in.at[0]
    )
    pair_db = across_core(lambda t: db_half.at[t], lambda s: db_got, 10, lambda n: db_got)
    pair_dc = across_core(lambda t: dc_half.at[t], lambda s: dc_got, 11, lambda n: dc_got)
    relay = Exchange(
        nc, my, lambda t: by_core(sibling),
        lambda s: pack_in.at[2 * s + core], lambda s: None, sems.at[12],
        lambda n: pack_in.at[:n],
    )

    def pack_copy(to, slot):
        return pltpu.make_async_remote_copy(
            src_ref=pack_out.at[to],
            dst_ref=pack_in.at[2 * slot + core],
            send_sem=pack_sems.at[0],
            recv_sem=pack_sems.at[1 + slot],
            device_id=by_chip(to),
            device_id_type=MESH,
        )

    def packs_sent():
        if nc > 1:
            pltpu.make_async_remote_copy(
                src_ref=pack_out.at[: nc - 1],
                dst_ref=pack_out.at[: nc - 1],
                send_sem=pack_sems.at[0],
                recv_sem=pack_sems.at[1],
                device_id=by_chip(my),
                device_id_type=MESH,
            ).wait_send()

    grads_a = Unit(0, 1, 0, 0, part, hh)
    grads_b = Unit(1, 1, 1, part, part, hh)
    states_a = Unit(2, 0, 0, 0, part, hh)
    states_b = Unit(3, 0, 1, part, part // 2, hh)
    states_c = Unit(4, 0, 1, part + part // 2, part // 2, hh)
    my_half = lax.rem(mz, 2)

    def rows_of(u, i):
        return pl.ds(pl.multiple_of(u.first + i * u.share, u.share), u.share)

    def my_rows(u):
        return rows_of(u, mz // 2)

    def to_scanner(u):
        return Exchange(
            nz, mz, by_z,
            lambda t: locals_ref.at[u.scan, rows_of(u, t // 2), :],
            lambda s: scan_in.at[u.index, s, : u.share, :],
            sems.at[13 + u.index],
            lambda n: scan_in.at[u.index, :n, : u.share, :],
        )

    def from_scanner(u):
        return Exchange(
            nz, mz, by_z,
            lambda t: turned.at[u.index, t, : u.share, :],
            lambda s: ends.at[u.scan, my_rows(u), :],
            sems.at[18 + u.index],
            lambda n: turned.at[u.index, :n, : u.share, :],
        )

    def ex_total(u):
        return Exchange(
            nx, mx, by_x,
            lambda t: total_send.at[u.index, : u.share, :],
            lambda s: total_in.at[u.index, s, : u.share, :],
            sems.at[23 + u.index],
            lambda n: total_in.at[u.index, :n, : u.share, :],
        )

    ex_decay = Exchange(
        nz, mz, by_z, lambda t: decay_out, lambda s: decay_in.at[s], sems.at[28],
        lambda n: decay_in.at[:n],
    )
    ex_line_decay = Exchange(
        nx, mx, by_x, lambda t: line_out, lambda s: line_in.at[s], sems.at[29],
        lambda n: line_in.at[:n],
    )

    def by_half(half, act):
        @pl.when(my_half == half)
        def _():
            if hh > 1:
                act(hh - 1)

        @pl.when(my_half != half)
        def _():
            act(hh)

    def scanners(half, act):
        for j in range(hh):
            i = lax.rem(mz // 2 + hh // 2 + j, hh)

            @pl.when(2 * i + half != mz)
            def _(z=2 * i + half):
                act(z)

    own_dy = pltpu.make_async_copy(columns(dy_ref)(me), block(dyg, tok)(me), own_sems.at[0])
    own_x = pltpu.make_async_copy(columns(x_ref)(me), block(xg, tok)(me), own_sems.at[1])
    for fetch in fetches:
        fetch.wait()
    padded = jnp.concatenate([step_ref[...], jnp.zeros((heads - tok, heads), F32)], axis=0)
    flipped = jnp.transpose(padded)
    for target in range(nc):
        g = target * 2 * hl // of_group
        pack_out[target, :tok, :] = write_ref[:, g * STATE : (g + 1) * STATE]
        pack_out[target, tok : 2 * tok, :] = read_ref[:, g * STATE : (g + 1) * STATE]
        first = target * 2 * hl
        pack_out[target, 2 * tok :, :heads] = flipped[first : first + hl, :] + pltpu.roll(
            flipped[first + hl : first + 2 * hl, :], tok, 1
        )
    pack_in[me] = pack_out[my]

    fetch_dy.wait()
    own_dy.start()
    fetch_x.wait()
    own_x.start()
    pl.semaphore_wait(barrier, (nh - 1) + (nz - 1) + (nx - 1))

    pair_pack.start(sibling)
    each(nc, my, lambda to: pack_copy(to, my).start())
    for exchange in (*ex_dy, ex_x[0]):
        exchange.start_all()

    def hand_on(chip):
        pack_copy(chip, chip).wait_recv()
        pltpu.make_async_remote_copy(
            src_ref=pack_in.at[2 * chip + core],
            dst_ref=pack_in.at[2 * chip + core],
            send_sem=sems.at[12, 0],
            recv_sem=sems.at[12, 1],
            device_id=by_core(sibling),
            device_id_type=MESH,
        ).start()

    each(nc, my, hand_on)
    for exchange in ex_x[1:]:
        exchange.start_all()
    pair_pack.arrived()
    relay.arrived()
    bg[...] = pack_in[:, :tok, :].reshape(total, STATE)
    cg[...] = pack_in[:, tok : 2 * tok, :].reshape(total, STATE)

    per_tile = heads // tok
    lane_h = lax.broadcasted_iota(jnp.int32, (hl, heads), 1) // tok
    tiles = []
    for first_source in range(0, nh, per_tile):
        tile = jnp.zeros((hl, heads), F32)
        for source in range(first_source, min(nh, first_source + per_tile)):
            spot = source - first_source
            piece = pack_in[source, 2 * tok :, :heads]
            both = []
            for c in range(2):
                shift = (heads + tok * (spot - c)) % heads
                both.append(pltpu.roll(piece, shift, 1) if shift else piece)
            tile = jnp.where(lane_h == spot, jnp.where(core == 0, both[0], both[1]), tile)
        tiles.append(tile)
    step = jnp.concatenate(tiles, axis=1)[:, :total]
    place = lax.broadcasted_iota(jnp.int32, (hl, 1), 0)
    rate = jnp.zeros((hl, 1), F32)
    for h in range(hl):
        rate = jnp.where(place == h, rate_ref[h], rate)
    lane = lax.broadcasted_iota(jnp.int32, (1, width), 1)
    skip = jnp.zeros((1, width), F32)
    for h in range(hl):
        skip = jnp.where(lane // WIDTH == h, skip_ref[h], skip)
    row_at = lax.broadcasted_iota(jnp.int32, (total, total), 0)
    col_at = lax.broadcasted_iota(jnp.int32, (total, total), 1)
    cumul = exact_nn(-step * rate, (col_at >= row_at).astype(F32))
    cum_ref[...] = cumul
    tail = jnp.exp(cumul[:, total - 1 : total])
    spread = (
        lax.broadcasted_iota(jnp.int32, (hl, width), 1) // WIDTH
        == lax.broadcasted_iota(jnp.int32, (hl, width), 0)
    ).astype(F32)
    wide = exact_tn(cumul, spread)
    wide_cum[...] = wide
    grow[...] = jnp.exp(wide)
    wide_weight[...] = jnp.exp(wide[total - 1 : total, :] - wide)
    wide_step[...] = exact_tn(step, spread)
    decay_out[...] = jnp.broadcast_to(tail, (hl, STATE))
    ex_decay.start_all()
    decay_in[mz] = decay_out[...]
    left_lanes = lax.broadcasted_iota(jnp.int32, (total, 2 * WIDTH), 1) < WIDTH
    later = lax.broadcasted_iota(jnp.int32, (low, low), 1) >= lax.broadcasted_iota(
        jnp.int32, (low, low), 0
    )

    def pair_cols(pair):
        return rows(pair, 2 * WIDTH)

    def masked(gap):
        return jnp.where(later, jnp.exp(jnp.where(later, gap, 0.0)), 0.0)

    def fill_decays(pair, carry):
        here = wide_cum[:, pair_cols(pair)]
        turned_round = pltpu.roll(here, WIDTH, 1)
        for side in range(2):
            h = 2 * pair + side
            col = jnp.where(left_lanes == (side == 0), here, turned_round)[:, :low]
            row = cum_ref[pl.ds(h, 1), :]
            decay_top[h, :, :low] = masked(row[:, :low] - col[:low, :])
            decay_top[h, :, low:] = jnp.exp(row[:, low:] - col[:low, :])
            decay_low[h] = masked(row[:, low:] - col[low:, :])
        return carry

    def send_local(u, local):
        locals_ref[u.scan, u.cut(), :] = local
        scanners(u.half, to_scanner(u).start)

        @pl.when(my_half == u.half)
        def _():
            scan_in[u.index, mz, : u.share, :] = locals_ref[u.scan, my_rows(u), :]

    def line_decays():
        ex_decay.arrived()
        product = decay_in[0]
        for z in range(1, nz):
            product = product * decay_in[z]
        line_out[...] = product
        line_in[mx] = product
        if nx > 1:
            ex_line_decay.start_all()

    def scan_line(u):
        @pl.when(my_half == u.half)
        def _():
            head = pl.ds((u.first + mz // 2 * u.share) // WIDTH, 1)
            to_scanner(u).arrived()
            state = jnp.zeros((u.share, STATE), F32)
            product = jnp.ones((1, STATE), F32)
            for lap in range(nz):
                z = nz - 1 - lap if u.scan else lap
                prefix[u.index, z, : u.share, :] = state
                products[u.index, z] = jnp.broadcast_to(product, (8, STATE))
                factor = decay_in[z, head, :]
                state = factor * state + scan_in[u.index, z, : u.share, :]
                product = product * factor
            total_send[u.index, : u.share, :] = state
            if nx > 1:
                ex_total(u).start_all()

    def scan_turn(u):
        @pl.when(my_half == u.half)
        def _():
            head = pl.ds((u.first + mz // 2 * u.share) // WIDTH, 1)
            state = jnp.zeros((u.share, STATE), F32)
            if nx > 1:
                total_in[u.index, mx, : u.share, :] = total_send[u.index, : u.share, :]
                ex_total(u).arrived()
                for lap in range(nx):
                    x = nx - 1 - lap if u.scan else lap
                    before = x > mx if u.scan else x < mx
                    moved = line_in[x, head, :] * state + total_in[u.index, x, : u.share, :]
                    state = jnp.where(before, moved, state)

            def turn(z):
                turned[u.index, z, : u.share, :] = (
                    prefix[u.index, z, : u.share, :] + products[u.index, z, :1, :] * state
                )

            def turn_to(z):
                turn(z)
                from_scanner(u).start(z)

            each(nz, mz, turn_to)
            turn(mz)
            ends[u.scan, my_rows(u), :] = turned[u.index, mz, : u.share, :]

    def scan_arrived(u):
        by_half(u.half, from_scanner(u).arrived)

    def scan_sent(u):
        by_half(u.half, to_scanner(u).sent)

        @pl.when(my_half == u.half)
        def _():
            ex_total(u).sent()
            from_scanner(u).sent()

    def send_grad(u):
        cols = u.cut()
        ex_dy[u.half].arrived()
        send_local(u, tn(grow[:, cols] * dyg[:, cols], cg[...]))

    def send_state(u):
        cols = u.cut()
        ex_x[u.index - 2].arrived()
        send_local(u, tn(wide_weight[:, cols] * wide_step[:, cols] * xg[:, cols], bg[...]))

    def send_dx(u):
        scan_arrived(u)
        cols = u.cut()
        whole = summed[:, cols] + wide_weight[:, cols] * nt(bg[...], ends[1, cols, :])
        summed[:, cols] = whole
        dx_buf[:, cols] = wide_step[:, cols] * whole + skip[:, cols] * dyg[:, cols]
        ex_dx[u.half].start_all()

    own_dy.wait()
    send_grad(grads_a)
    score_top[...] = nt(bg[:low, :], cg[...])
    score_low[...] = nt(bg[low:, :], cg[low:, :])
    lax.fori_loop(0, pairs, fill_decays, 0)

    def fill_summed(pair, carry):
        cols = pair_cols(pair)
        grads = dyg[:, cols]
        heads_of = (2 * pair, 2 * pair + 1)
        above = nn(
            jnp.concatenate([score_top[...] * decay_top[h] for h in heads_of], axis=0), grads
        )
        below = nn(
            jnp.concatenate([score_low[...] * decay_low[h] for h in heads_of], axis=0),
            grads[low:, :],
        )
        summed[:low, cols] = jnp.where(left_lanes[:low, :], above[:low, :], above[low:, :])
        summed[low:, cols] = jnp.where(left_lanes[:low, :], below[:low, :], below[low:, :])
        return carry

    def fill_grad_score(pair, carry):
        cols = pair_cols(pair)
        grads = dyg[:, cols]
        scaled = wide_step[:, cols] * xg[:, cols]
        sides = [jnp.where(left_lanes == (side == 0), scaled, 0.0) for side in range(2)]
        above = nt(jnp.concatenate([one[:low, :] for one in sides], axis=0), grads)
        below = nt(jnp.concatenate([one[low:, :] for one in sides], axis=0), grads[low:, :])
        mixed_top, mixed_low = [], []
        for side in range(2):
            h = 2 * pair + side
            mixed_top.append(above[side * low : (side + 1) * low, :] * decay_top[h])
            mixed_low.append(below[side * low : (side + 1) * low, :] * decay_low[h])
            sums = jnp.sum(mixed_top[side] * score_top[...], axis=0, keepdims=True)
            more = jnp.sum(mixed_low[side] * score_low[...], axis=0, keepdims=True)
            mine = lax.broadcasted_iota(jnp.int32, (hl, low), 0) == h
            row_sums[:, :low] += jnp.where(mine, sums[:, :low], 0.0)
            row_sums[:, low:] += jnp.where(mine, sums[:, low:] + more, 0.0)
        grad_top[...] += mixed_top[0] + mixed_top[1]
        grad_low[...] += mixed_low[0] + mixed_low[1]
        return carry

    grad_top[...] = jnp.zeros_like(grad_top)
    grad_low[...] = jnp.zeros_like(grad_low)
    row_sums[...] = jnp.zeros_like(row_sums)
    line_decays()
    send_grad(grads_b)
    lax.fori_loop(0, pairs // 2, fill_summed, 0)
    scan_line(grads_a)
    own_x.wait()
    send_state(states_a)
    send_state(states_b)
    send_state(states_c)
    if nx > 1:
        ex_line_decay.arrived()
    scan_turn(grads_a)
    scan_line(grads_b)
    lax.fori_loop(pairs // 2, pairs, fill_summed, 0)
    scan_turn(grads_b)
    scan_line(states_a)
    scan_line(states_b)
    scan_line(states_c)
    scan_turn(states_a)
    send_dx(grads_a)
    lax.fori_loop(0, pairs // 2, fill_grad_score, 0)
    scan_turn(states_b)
    scan_turn(states_c)
    send_dx(grads_b)
    lax.fori_loop(pairs // 2, pairs, fill_grad_score, 0)
    end = ends[1]

    def by_target_core(half, stride, first, value):
        size = value.shape[0] // nh
        for target in range(nh):
            base = (target // 2) * stride + first
            half[target % 2, base : base + size, :] = value[target * size : (target + 1) * size, :]

    from_states = nn(wide_weight[...] * wide_step[...] * xg[...], end)
    by_target_core(db_half, tok, 0, from_states + jnp.concatenate(
        [nn(grad_top[...], cg[...]), nn(grad_low[...], cg[low:, :])], axis=0
    ))
    pair_db.start(sibling)
    along = sum_nt(spread, xg[...] * summed[...])
    from_score = jnp.concatenate(
        [
            tn(grad_top[:, :low], bg[:low, :]),
            tn(grad_top[:, low:], bg[:low, :]) + tn(grad_low[...], bg[low:, :]),
        ],
        axis=0,
    )
    outer = grow[...] * dyg[...]
    made = jnp.sum((end * locals_ref[0]).reshape(hl, WIDTH, STATE), axis=1)
    read_part = from_score
    along_read = row_sums[...] - step * along
    kept = []
    for u in (states_a, states_b, states_c):
        if u is states_b:
            pair_db.arrived()
            db_sum[...] = db_half[core] + db_got[...]
            ex_db.start_all()
            db_in[rows(my, tok), :] = db_sum[rows(my, tok), :]
        scan_arrived(u)
        start = ends[0, u.cut(), :]
        kept.append(
            jnp.sum((end[u.cut(), :] * start).reshape(u.count // WIDTH, WIDTH, STATE), axis=1)
        )
        read_part = read_part + nn(outer[:, u.cut()], start)
        along_read = along_read + sum_nt(
            spread[:, u.cut()], outer[:, u.cut()] * nt(cg[...], start)
        )
    by_target_core(dc_half, tail_rows, 0, read_part)
    kept = jnp.concatenate(kept, axis=0)
    last = jnp.sum(tail * kept + made, axis=1, keepdims=True)
    lane_t = lax.broadcasted_iota(jnp.int32, (hl, total), 1)
    grad_cum = along_read + jnp.where(lane_t == total - 1, last, 0.0)
    grad_log = exact_nn(grad_cum, (row_at >= col_at).astype(F32))
    grad_step = along - rate * grad_log
    for begin in range(0, total, heads):
        piece = grad_step[:, begin : min(total, begin + heads)]
        if piece.shape[1] < heads:
            piece = jnp.concatenate(
                [piece, jnp.zeros((hl, heads - piece.shape[1]), F32)], axis=1
            )
        turns = [pltpu.roll(piece, tok * t, 1) if t else piece for t in range(per_tile)]
        for spot in range(min(per_tile, nh)):
            target = begin // tok + spot
            placed = [turns[(c - spot) % per_tile] for c in range(2)]
            base = (target // 2) * tail_rows + tok
            dc_half[target % 2, base : base + hl, :heads] = jnp.where(
                lane_h == core, jnp.where(core == 0, placed[0], placed[1]), 0.0
            )
    pair_dc.start(sibling)
    pair_dc.arrived()
    dc_sum[...] = dc_half[core] + dc_got[...]
    ex_dc.start_all()
    dc_in[rows(my, tail_rows), :] = dc_sum[rows(my, tail_rows), :]

    share = nc // groups

    def fold(received, stride, out):
        for g in range(groups):
            part = received[g * share * stride : g * share * stride + tok, :]
            for s in range(g * share + 1, (g + 1) * share):
                part = part + received[s * stride : s * stride + tok, :]
            out[:, g * STATE : (g + 1) * STATE] = part

    own_dx = pltpu.make_async_copy(block(dx_buf, tok)(me), columns(dx_ref)(me), own_sems.at[2])
    own_dx.start()
    for exchange in (*ex_dy, *ex_x, *ex_dx, relay, ex_decay, ex_line_decay):
        exchange.sent()
    packs_sent()
    for u in (grads_a, grads_b, states_a, states_b, states_c):
        scan_sent(u)
    for exchange in (pair_pack, pair_db, pair_dc):
        exchange.sent()
    for exchange in ex_dx:
        exchange.arrived()
    ex_db.arrived()
    fold(db_in, tok, dwrite_ref)
    ex_db.sent()
    ex_dc.arrived()
    fold(dc_in, tail_rows, dread_ref)
    by_heads = []
    for chip in range(nc):
        piece = dc_in[chip * tail_rows + tok : (chip + 1) * tail_rows, :heads]
        by_heads += [piece, pltpu.roll(piece, heads - tok, 1)]
    dstep_ref[...] = jnp.transpose(jnp.concatenate(by_heads, axis=0))[:tok, :]
    ex_dc.sent()
    own_dx.wait()


def hand_out(parts, *refs):
    count = len(parts)
    sems = refs[-1]
    copies = []
    for i in range(count):
        wide = refs[i].shape[1] // parts[i]
        for p in range(parts[i]):
            cols = slice(p * wide, (p + 1) * wide)
            copies.append(
                pltpu.make_async_copy(
                    refs[i].at[:, cols], refs[count + i].at[:, cols], sems.at[len(copies)]
                )
            )
    for copy in copies:
        copy.start()
    for copy in copies:
        copy.wait()


def on_device(groups, features, write_proj, read_proj, step_size, decay_rate, skip_weight, upstream):
    nh = lax.axis_size("head")
    tok, heads = step_size.shape
    hl = heads // nh
    nz = hl
    nx = lax.axis_size("ctx") // nz
    width = hl * WIDTH
    nc = nh // 2
    total = nh * tok
    low = total // 2
    vmem = pl.BlockSpec(memory_space=pltpu.VMEM)
    hbm = pl.BlockSpec(memory_space=pltpu.HBM)

    def buf(*shape):
        return pltpu.VMEM(shape, F32)

    results = pl.pallas_call(
        functools.partial(kernel, nh, nx, nz, groups),
        out_shape=(
            jax.ShapeDtypeStruct(features.shape, F32),
            jax.ShapeDtypeStruct(write_proj.shape, F32),
            jax.ShapeDtypeStruct(read_proj.shape, F32),
            jax.ShapeDtypeStruct(step_size.shape, F32),
        ),
        in_specs=[hbm] * 7,
        out_specs=(vmem, vmem, vmem, vmem),
        scratch_shapes=[
            pltpu.SMEM(decay_rate.shape, F32),
            pltpu.SMEM(skip_weight.shape, F32),
            buf(*write_proj.shape),
            buf(*read_proj.shape),
            buf(*step_size.shape),
            buf(*features.shape),
            buf(*upstream.shape),
            buf(total, width),
            buf(total, width),
            buf(total, STATE),
            buf(total, STATE),
            buf(nc, 2 * tok + hl, STATE),
            buf(nh, 2 * tok + hl, STATE),
            buf(hl, total),
            buf(total, width),
            buf(total, width),
            buf(total, width),
            buf(total, width),
            buf(hl, low, total),
            buf(hl, low, low),
            buf(low, total),
            buf(low, low),
            buf(low, total),
            buf(low, low),
            buf(hl, total),
            buf(total, width),
            buf(total, width),
            buf(2, hl * WIDTH, STATE),
            buf(5, nz, WIDTH, STATE),
            buf(5, WIDTH, STATE),
            buf(5, nx, WIDTH, STATE),
            buf(5, nz, WIDTH, STATE),
            buf(5, nz, 8, STATE),
            buf(5, nz, WIDTH, STATE),
            buf(2, hl * WIDTH, STATE),
            buf(hl, STATE),
            buf(nz, hl, STATE),
            buf(hl, STATE),
            buf(nx, hl, STATE),
            buf(2, nc * tok, STATE),
            buf(nc * tok, STATE),
            buf(nc * tok, STATE),
            buf(nc * tok, STATE),
            buf(2, nc * (tok + hl), STATE),
            buf(nc * (tok + hl), STATE),
            buf(nc * (tok + hl), STATE),
            buf(nc * (tok + hl), STATE),
            pltpu.SemaphoreType.DMA((30, 2)),
            pltpu.SemaphoreType.DMA((1 + nc,)),
            pltpu.SemaphoreType.DMA((10,)),
        ],
        compiler_params=pltpu.CompilerParams(
            collective_id=0, has_side_effects=True, vmem_limit_bytes=40 * 1024 * 1024
        ),
        cost_estimate=pl.CostEstimate(
            flops=1_200_000_000, bytes_accessed=8_000_000, transcendentals=600_000
        ),
    )(
        *(
            pltpu.with_memory_space_constraint(a, pltpu.HBM)
            for a in (
                decay_rate, skip_weight, features, upstream, write_proj, read_proj, step_size
            )
        )
    )
    parts = (4, 1, 1, 1)
    return pl.pallas_call(
        functools.partial(hand_out, parts),
        out_shape=tuple(jax.ShapeDtypeStruct(r.shape, F32) for r in results),
        in_specs=[vmem] * len(results),
        out_specs=(hbm,) * len(results),
        scratch_shapes=[pltpu.SemaphoreType.DMA((sum(parts),))],
        compiler_params=pltpu.CompilerParams(vmem_limit_bytes=16 * 1024 * 1024),
        cost_estimate=pl.CostEstimate(flops=0, bytes_accessed=1_200_000, transcendentals=0),
    )(*(pltpu.with_memory_space_constraint(r, pltpu.VMEM) for r in results))


def solution(mesh):
    tokens = P(("ctx", "head"), None)
    return jax.shard_map(
        functools.partial(on_device, GROUPS),
        mesh=mesh,
        in_specs=(tokens, tokens, tokens, tokens, P("head"), P("head"), tokens),
        out_specs=(tokens, tokens, tokens, tokens),
        check_vma=False,
    )
```
